32 devices in a mesh: section: 2 (over x), dp: 16 (over z, y, core).
Axes of the slice: x: 2, y: 2, z: 4, core: 2. Of those that a mesh axis runs over, the one named last changes fastest.
Arguments:
- ends: float32 [2, 2, 4096, 768], P('section', None, 'dp'), may hold values from -6 to 6
- lengths: int32 [2, 16, 3], P(None, 'dp'), may hold values from 22 to 197, as said below
- norm_gains: float32 [2, 2, 768], P('section'), may hold values from 0.1 to 1.9
- norm_shifts: float32 [2, 2, 768], P('section'), may hold values from -3 to 3
- attend_weight: bfloat16 [2, 768, 2304], P('section'), may hold values from -0.21875 to 0.21875
- offsets: float32 [2, 4, 768], P('section'), may hold values from -3 to 3
- output_weight: bfloat16 [2, 768, 768], P('section'), may hold values from -0.875 to 0.875
- expand_weight: bfloat16 [2, 768, 3072], P('section'), may hold values from -0.21875 to 0.21875
- expand_bias: float32 [2, 3072], P('section'), may hold values from -3 to 3
- reduce_weight: bfloat16 [2, 3072, 768], P('section'), may hold values from -0.109375 to 0.109375
Outputs:
- boundary: float32 [2, 2, 4096, 768], P('section', None, 'dp')
- gain_grads: float32 [2, 2, 768], P('section', None, 'dp')
- shift_grads: float32 [2, 2, 768], P('section', None, 'dp')
- attend_grads: float32 [2, 768, 2304], P('section', None, 'dp')
- offset_grads: float32 [2, 4, 768], P('section', None, 'dp')
- output_grads: float32 [2, 768, 768], P('section', None, 'dp')
- expand_grads: float32 [2, 768, 3072], P('section', None, 'dp')
- bias_grads: float32 [2, 3072], P('section', 'dp')
- reduce_grads: float32 [2, 3072, 768], P('section', None, 'dp')
The draws below stay inside these ranges and needn't reach their ends.
Inputs may be any that keep to these rules, and one draw needn't show every extreme that they name: `lengths`: each row of 3 counts holds, in an order drawn for that row, one count 197, 1 counts 37 and one count 256 - 197 - 1 * 37; a row sums to 256.
All inputs are finite; a program needn't handle non-finite values.
Results may differ from the reference program's by a relative error of at most 0.012.
Values may be sent and summed in bfloat16 or wider, within the bound.
No kernel may reach another device: no remote copies, remote signals or barrier semaphores. Data moves between devices by JAX's collectives and lax.ppermute only.
A program may use at most 256 MiB of HBM per device.

```python
import jax
import jax.numpy as jnp
from jax import lax

D = 768
HEADS = 12
FF = 3072
HEAD_DIM = 64
TOK_MB = 256
MICRO = 2
LOCALS = 1
GLOBAL_LEN = 197
LOCAL_LEN = 37
CROPS = 3
TOKENS = 4096
N_DP = 16


def draw_lengths(key, part):
    key = jax.random.fold_in(key, 7)
    filler = TOK_MB - GLOBAL_LEN - LOCALS * LOCAL_LEN
    profile = jnp.concatenate([jnp.full((1,), GLOBAL_LEN, jnp.int32), jnp.full((LOCALS,), LOCAL_LEN, jnp.int32), jnp.full((1,), filler, jnp.int32)])
    scores = jax.random.randint(key, (MICRO, N_DP, CROPS), 0, 1 << 20, dtype=jnp.int32) * CROPS
    scores = scores + jnp.arange(CROPS, dtype=jnp.int32)
    order = jnp.argsort(scores, axis=-1)
    return profile[order].astype(jnp.int32)


def raised(drawn, own_key, source, target, blocks, factor):
    def block_of(position):
        return (jnp.arange(drawn.shape[position]) // (drawn.shape[position] // blocks)).reshape((-1,) + (1,) * (drawn.ndim - 1 - position))

    near = jax.random.permutation(own_key, blocks)[block_of(target)]
    far = (block_of(target) + blocks // 2) % blocks
    return jnp.where((block_of(source) == near) | (block_of(source) == far), factor * drawn, drawn)


def level_of(stream_key, extent, cuts, smallest, top_value):
    loudness = 1.0
    for position, parts in cuts:
        draws = jax.random.uniform(jax.random.fold_in(jax.random.fold_in(stream_key, 6), position), (parts,), jnp.float32, smallest / len(cuts), top_value / len(cuts))
        loudness = loudness * jnp.repeat(jnp.exp(draws), extent[position] // parts).reshape((-1,) + (1,) * (len(extent) - 1 - position))
    return loudness


def normal_values(key, dims, width, limit, shards=(), held_as=jnp.bfloat16):
    level = level_of(key, dims, shards, -0.22, 0.18) if shards else 1.0
    values = jax.random.normal(key, dims, jnp.float32) * width * level
    return jnp.minimum(jnp.maximum(values, -limit), limit).astype(held_as)


def gaussian_with(stream_key, extent, deviation, bound, pieces, heavy, kind=jnp.bfloat16):
    result = deviation * jax.random.normal(stream_key, extent, jnp.float32)
    if pieces:
        result = result * level_of(stream_key, extent, pieces, -0.22, 0.18)
    return jnp.clip(raised(result, jax.random.fold_in(stream_key, 3), *heavy), -bound, bound).astype(kind)


def setup_inputs(seed: int = 0) -> dict:
    key_list = jax.random.split(jax.random.key(seed), 11)
    ends = gaussian_with(key_list[0], (2, MICRO, TOKENS, D), 1.0, 6.0, ((0, 2), (2, 16)), (2, 3, 16, 2.0), jnp.float32)
    lengths = draw_lengths(jax.random.fold_in(key_list[10], 71), 0)
    norm_gains = jnp.clip(1.0 + 0.18 * jax.random.normal(key_list[2], (2, 2, D), jnp.float32), 0.1, 1.9)
    norm_shifts = normal_values(key_list[3], (2, 2, D), 0.5, 3.0, ((0, 2),), jnp.float32)
    attend_weight = normal_values(key_list[4], (2, D, 3 * D), D ** -0.5, 0.21875, ((0, 2),))
    offsets = normal_values(key_list[5], (2, 4, D), 0.5, 3.0, ((0, 2),), jnp.float32)
    output_weight = normal_values(key_list[6], (2, D, D), (D // 16) ** -0.5, 0.875, ((0, 2),))
    expand_weight = normal_values(key_list[7], (2, D, FF), D ** -0.5, 0.21875, ((0, 2),))
    expand_bias = normal_values(key_list[8], (2, FF), 0.5, 3.0, ((0, 2),), jnp.float32)
    reduce_weight = normal_values(key_list[9], (2, FF, D), FF ** -0.5, 0.109375, ((0, 2),))
    return dict(ends=ends, lengths=lengths, norm_gains=norm_gains, norm_shifts=norm_shifts, attend_weight=attend_weight, offsets=offsets, output_weight=output_weight, expand_weight=expand_weight, expand_bias=expand_bias, reduce_weight=reduce_weight)


@jax.custom_vjp
def low(v):
    return lax.optimization_barrier(v.astype(jnp.bfloat16)).astype(jnp.float32)

@jax.custom_vjp
def low_back(v):
    return v

def low_keep(v):
    return (low(v), None)

def low_pass(kept, grad):
    return (grad,)

def back_keep(v):
    return (v, None)

def back_low(kept, grad):
    return (low(grad),)
low.defvjp(low_keep, low_pass)
low_back.defvjp(back_keep, back_low)

def norm_rows(values, gain, shift):
    center = values - lax.optimization_barrier(jnp.mean(values, axis=-1, keepdims=True))
    spread = lax.optimization_barrier(jnp.mean(center * center, axis=-1, keepdims=True))
    return center * lax.rsqrt(spread + 1e-06) * gain + shift

def segment_ids(counts, count_rows):
    bounds = jnp.cumsum(counts, dtype=jnp.int32)
    spots = jnp.arange(count_rows, dtype=jnp.int32)
    return lax.optimization_barrier(jnp.sum((spots[:, None] >= bounds[None, :]).astype(jnp.int32), axis=1, dtype=jnp.int32))

def layer_block(inputs, segment, params):
    gains, shifts, attend_weight, offsets, output_weight, expand_weight, expand_bias, reduce_weight = params
    highest = lax.Precision.HIGHEST
    count_rows = inputs.shape[0]
    first = low(norm_rows(inputs, gains[0], shifts[0]))
    joined = jnp.dot(first, attend_weight, precision=highest)
    query = low_back(low(joined[:, :D] + offsets[0])).reshape(count_rows, HEADS, HEAD_DIM)
    keys = low_back(low(joined[:, D:2 * D])).reshape(count_rows, HEADS, HEAD_DIM)
    values = low_back(low(joined[:, 2 * D:] + offsets[1])).reshape(count_rows, HEADS, HEAD_DIM)
    scores = low_back(jnp.einsum('qhd,khd->hqk', query, keys, precision=highest) * HEAD_DIM ** (-0.5))
    scores = jnp.where((segment[:, None] == segment[None, :])[None], scores, -1e+30)
    probs = low(jax.nn.softmax(scores, axis=-1))
    mixed = jnp.einsum('hqk,khd->qhd', probs, values, precision=highest).reshape(count_rows, D)
    mixed = low_back(low(mixed))
    resid = inputs + low_back(jnp.dot(mixed, output_weight, precision=highest)) + offsets[2]
    second = low(norm_rows(resid, gains[1], shifts[1]))
    pre = low_back(jnp.dot(second, expand_weight, precision=highest)) + expand_bias
    act = low(jax.nn.gelu(pre, approximate=False))
    return resid + low_back(jnp.dot(act, reduce_weight, precision=highest)) + offsets[3]

def run_layer(blocks, segments, params):
    single = jax.checkpoint(lambda inputs, segment: layer_block(inputs, segment, params))
    return lax.map(lambda pair: single(pair[0], pair[1]), (blocks, segments))

def reference(ends, lengths, norm_gains, norm_shifts, attend_weight, offsets, output_weight, expand_weight, expand_bias, reduce_weight):
    count_blocks = MICRO * N_DP
    inputs = ends[0].reshape(count_blocks, TOK_MB, D)
    cotangent = ends[1].reshape(count_blocks, TOK_MB, D)
    segments = jax.vmap(lambda counts: segment_ids(counts, TOK_MB))(lengths.reshape(count_blocks, CROPS))
    params = (norm_gains, norm_shifts, attend_weight.astype(jnp.float32), offsets, output_weight.astype(jnp.float32), expand_weight.astype(jnp.float32), expand_bias, reduce_weight.astype(jnp.float32))

    def forward(start, weights):
        layer_zero = tuple((w[0] for w in weights))
        layer_one = tuple((w[1] for w in weights))
        middle = low_back(low(run_layer(start, segments, layer_zero)))
        return run_layer(middle, segments, layer_one)
    outputs, pullback = jax.vjp(forward, inputs, params)
    grad_in, grads = pullback(cotangent)
    boundary = jnp.stack([grad_in.reshape(MICRO, TOKENS, D), outputs.reshape(MICRO, TOKENS, D)])
    return (boundary, grads[0], grads[1], grads[2], grads[3], grads[4], grads[5], grads[6], grads[7])
```

```python
import functools
import jax
import jax.numpy as jnp
from jax import lax
from jax.experimental import pallas as pl
from jax.experimental.pallas import tpu as pltpu
from jax.sharding import PartitionSpec as P

HEADS = 12
ROWS = 32
BF = jnp.bfloat16
F32 = jnp.float32
VM = pl.BlockSpec(memory_space=pltpu.VMEM)
SM = pl.BlockSpec(memory_space=pltpu.SMEM)
HB = pl.BlockSpec(memory_space=pltpu.HBM)
ANY = pl.BlockSpec(memory_space=pl.ANY)


def in_hbm(value):
    return pltpu.with_memory_space_constraint(value, pltpu.HBM)


def pinned(value):
    return pltpu.with_memory_space_constraint(value, pltpu.VMEM)


def dot(left, right, dims=((1,), (0,))):
    return lax.dot_general(left, right, (dims, ((), ())), preferred_element_type=F32)


def dot_nt(left, right):
    return dot(left, right, ((1,), (1,)))


def dot_tn(left, right):
    return dot(left, right, ((0,), (0,)))


def group_bias(lengths_ref, micro, count):
    rows = lax.broadcasted_iota(jnp.int32, (count, count), 0)
    cols = lax.broadcasted_iota(jnp.int32, (count, count), 1)
    bound = jnp.int32(0)
    row_group = jnp.zeros((count, count), jnp.int32)
    col_group = jnp.zeros((count, count), jnp.int32)
    for crop in range(lengths_ref.shape[2]):
        bound = bound + lengths_ref[micro, 0, crop]
        row_group = row_group + (rows >= bound).astype(jnp.int32)
        col_group = col_group + (cols >= bound).astype(jnp.int32)
    return jnp.where(row_group == col_group, 0.0, -1e30).astype(F32)


def gelu_parts(pre):
    size = jnp.abs(pre) * (2.0 ** -0.5)
    bell = jnp.exp(-size * size)
    t = 1.0 / (1.0 + 0.3275911 * size)
    poly = t * (0.254829592 + t * (-0.284496736 + t * (1.421413741 + t * (-1.453152027 + t * 1.061405429))))
    tail = 0.5 * poly * bell
    upper = jnp.where(pre >= 0, 1.0 - tail, tail)
    return pre * upper, upper + pre * (bell * 0.3989422804014327)


def norm_rows(values):
    center = values - jnp.mean(values, axis=-1, keepdims=True)
    factor = lax.rsqrt(jnp.mean(center * center, axis=-1, keepdims=True) + 1e-06)
    return center * factor, factor


def halves(count):
    lane = lax.broadcasted_iota(jnp.int32, (count, 128), 1)
    return lane < 64, lane >= 64


def forward_body(
    micro, lengths_ref, gains, shifts, offsets, bias, a, attend_v, output_v, expand_v, reduce_v, ready,
    first, joined, probs, mixed, unit, unit_two, factors, second, act, slope, resid, low, mask,
):
    count, width = a.shape
    hidden = act.shape[1]
    mask[...] = group_bias(lengths_ref, micro, count)
    gain, shift = gains[0, 0:1, :], shifts[0, 0:1, :]
    for r in range(0, count, ROWS):
        rows = pl.ds(r, ROWS)
        normed, factor = norm_rows(a[rows, :])
        unit[rows, :] = normed
        factors[rows, 0:1] = factor
        first[rows, :] = (normed * gain + shift).astype(BF)

    for i in range(3):
        ready("attend", i)
        cols = pl.ds(i * width, width)
        part = dot(first[...], attend_v[:, cols])
        if i == 0:
            part = part + offsets[0, 0:1, :]
        if i == 2:
            part = part + offsets[0, 1:2, :]
        joined[:, cols] = part.astype(BF)

    sides = halves(count)
    for pair in range(HEADS // 2):
        query = joined[:, pl.ds(pair * 128, 128)] * (64 ** -0.5)
        key = joined[:, pl.ds(width + pair * 128, 128)]
        value = joined[:, pl.ds(2 * width + pair * 128, 128)]
        total = None
        for half in range(2):
            scores = dot_nt(jnp.where(sides[half], query, 0).astype(BF), key) + mask[...]
            weights = jnp.exp(scores - jnp.max(scores, axis=-1, keepdims=True))
            prob = (weights * (1.0 / jnp.sum(weights, axis=-1, keepdims=True))).astype(BF)
            probs[2 * pair + half] = prob
            term = dot(prob, jnp.where(sides[half], value, 0).astype(BF))
            total = term if total is None else total + term
        mixed[:, pl.ds(pair * 128, 128)] = total.astype(BF)

    ready("output", 0)
    resid[...] = a[...] + dot(mixed[...], output_v[...]) + offsets[0, 2:3, :]
    gain, shift = gains[0, 1:2, :], shifts[0, 1:2, :]
    for r in range(0, count, ROWS):
        rows = pl.ds(r, ROWS)
        normed, factor = norm_rows(resid[rows, :])
        unit_two[rows, :] = normed
        factors[rows, 1:2] = factor
        second[rows, :] = (normed * gain + shift).astype(BF)

    for i in range(hidden // width):
        cols = pl.ds(i * width, width)
        ready("expand", i)
        pre = dot(second[...], expand_v[:, cols]) + bias[0:1, cols]
        value, grad = gelu_parts(pre)
        act[:, cols] = value.astype(BF)
        slope[:, cols] = grad.astype(BF)
        ready("reduce", i)
        resid[...] += dot(act[:, cols], reduce_v[cols, :])
    resid[...] += offsets[0, 3:4, :]
    low[...] = resid[...].astype(BF)


def first_kernel(
    where_ref, lengths_ref, gains, shifts, offsets, bias, ends, attend_w, output_w, expand_w, reduce_w, *rest
):
    *kept, attend_v, output_v, expand_v, reduce_v, a, mask, in_sem, sems = rest
    width = a.shape[1]
    hidden = bias.shape[1]
    source = pltpu.make_async_copy(ends.at[0, 0], a, in_sem)
    source.start()
    copies, number = {}, 0
    for i in range(3):
        cols = pl.ds(i * width, width)
        copies["attend", i] = attend_w.at[0, :, cols], attend_v.at[:, cols]
    copies["output", 0] = output_w.at[0], output_v
    for i in range(hidden // width):
        cols = pl.ds(i * width, width)
        copies["expand", i] = expand_w.at[0, :, cols], expand_v.at[:, cols]
        copies["reduce", i] = reduce_w.at[0, cols], reduce_v.at[cols]
    for number, (name, pair) in enumerate(copies.items()):
        copies[name] = pltpu.make_async_copy(*pair, sems.at[number])
        copies[name].start()
    source.wait()

    @pl.when(where_ref[0] == 0)
    def _():
        forward_body(
            where_ref[1], lengths_ref, gains, shifts, offsets, bias, a, attend_v, output_v, expand_v, reduce_v,
            lambda name, i: copies[name, i].wait(), *kept, mask,
        )

    @pl.when(where_ref[0] != 0)
    def _():
        for copy in copies.values():
            copy.wait()


def later_kernel(
    own, only, where_ref, lengths_ref, gains, shifts, offsets, bias, ends, incoming,
    attend_v, output_v, expand_v, reduce_v, *rest
):
    *kept, a, mask, in_sem = rest
    kept = kept[-12:]
    section = where_ref[0]

    def run():
        @pl.when(section == 0)
        def _():
            copy = pltpu.make_async_copy(ends.at[0, min(own, ends.shape[1] - 1)], a, in_sem)
            copy.start()
            copy.wait()

        @pl.when(section != 0)
        def _():
            a[...] = incoming[...].astype(F32)

        forward_body(
            where_ref[1 + own], lengths_ref, gains, shifts, offsets, bias, a, attend_v, output_v, expand_v, reduce_v,
            lambda name, i: None, *kept, mask,
        )

    if only:
        pl.when(section != 0)(run)
    else:
        run()


def kept_shapes(count, width, hidden):
    return [
        ((count, width), BF), ((count, 3 * width), BF), ((HEADS, count, count), BF), ((count, width), BF),
        ((count, width), F32), ((count, width), F32), ((count, 128), F32), ((count, width), BF),
        ((count, hidden), BF), ((count, hidden), BF), ((count, width), F32), ((count, width), BF),
    ]


LIMIT = 14 * 2**20


def forward_first(where, lengths, small, ends, weights):
    count, width = ends.shape[2:]
    hidden = small[3].shape[1]
    shapes = kept_shapes(count, width, hidden) + [(w.shape[1:], BF) for w in weights]
    out = pl.pallas_call(
        first_kernel,
        out_shape=[pltpu.VMEM(*s) for s in shapes],
        in_specs=[SM, SM] + [VM] * 4 + [HB] * 5,
        out_specs=[VM] * len(shapes),
        scratch_shapes=[
            pltpu.VMEM((count, width), F32), pltpu.VMEM((count, count), F32),
            pltpu.SemaphoreType.DMA, pltpu.SemaphoreType.DMA((4 + 2 * (hidden // width),)),
        ],
        compiler_params=pltpu.CompilerParams(vmem_limit_bytes=LIMIT),
        name="forward_first",
    )(where, lengths, *small, in_hbm(ends), *[in_hbm(w) for w in weights])
    return out[:12], out[12:]


def forward_later(own, where, lengths, small, ends, incoming, weights, slot=None):
    count, width = ends.shape[2:]
    hidden = small[3].shape[1]
    shapes = kept_shapes(count, width, hidden)
    slot = [] if slot is None else [pinned(s) for s in slot]
    return pl.pallas_call(
        functools.partial(later_kernel, own, bool(slot)),
        out_shape=[pltpu.VMEM(*s) for s in shapes],
        in_specs=[SM, SM] + [VM] * 4 + [HB] + [VM] * (5 + len(slot)),
        out_specs=[VM] * len(shapes),
        scratch_shapes=[pltpu.VMEM((count, width), F32), pltpu.VMEM((count, count), F32), pltpu.SemaphoreType.DMA],
        input_output_aliases={12 + i: i for i in range(len(slot))},
        compiler_params=pltpu.CompilerParams(vmem_limit_bytes=LIMIT),
        name="forward_later",
    )(where, lengths, *small, in_hbm(ends), pinned(incoming), *[pinned(w) for w in weights], *slot)


def norm_back_rows(grad, gain, normed, factor):
    scaled = grad * gain
    return factor * (
        scaled
        - jnp.mean(scaled, axis=-1, keepdims=True)
        - normed * jnp.mean(scaled * normed, axis=-1, keepdims=True)
    )


def column_sum(values):
    return jnp.sum(values, axis=0, keepdims=True)


def norm_back_all(grad, gain, normed_ref, factors, column, base, emit):
    count, width = normed_ref.shape
    gain_sum = jnp.zeros((8, width), F32)
    shift_sum = jnp.zeros((8, width), F32)
    result_sum = jnp.zeros((8, width), F32)

    def fold(values):
        return jnp.sum(values.reshape(-1, 8, width), axis=0)

    for r in range(0, count, ROWS):
        rows = pl.ds(r, ROWS)
        part, normed = grad[rows, :], normed_ref[rows, :]
        gain_sum = gain_sum + fold(part * normed)
        shift_sum = shift_sum + fold(part)
        result = base(rows) + norm_back_rows(part, gain, normed, factors[rows, column : column + 1])
        result_sum = result_sum + fold(result)
        emit(rows, result)
    return column_sum(gain_sum), column_sum(shift_sum), column_sum(result_sum)


def backward_outer(
    gains, g, unit_two, factors, slope, output_v, expand_v, reduce_v,
    g_low, pre_low, resid_low, grad_resid, grad_mixed, sums, grad_second,
):
    count, width = g.shape
    hidden = slope.shape[1]
    g_low[...] = g[...].astype(BF)
    sums[3:4, :] = column_sum(g[...])
    for i in range(hidden // width):
        cols = pl.ds(i * width, width)
        grad_pre = dot_nt(g_low[...], reduce_v[cols, :]) * slope[:, cols].astype(F32)
        sums[4 + i : 5 + i, :] = column_sum(grad_pre)
        pre_low[:, cols] = grad_pre.astype(BF)
        term = dot_nt(pre_low[:, cols], expand_v[:, cols])
        if i == 0:
            grad_second[...] = term
        else:
            grad_second[...] += term

    def emit(rows, result):
        grad_resid[rows, :] = result
        resid_low[rows, :] = result.astype(BF)

    sums[0:1, :], sums[1:2, :], sums[2:3, :] = norm_back_all(
        grad_second, gains[0, 1:2, :], unit_two, factors, 1, lambda rows: g[rows, :], emit
    )
    grad_mixed[...] = dot_nt(resid_low[...], output_v[...]).astype(BF)


def backward_inner(
    gains, grad_resid, grad_mixed, joined, probs, unit, factors, attend_v, grad_joined, grad_in, low, sums, grad_first
):
    count, width = grad_resid.shape
    sides = halves(count)
    for pair in range(HEADS // 2):
        at = [pl.ds(j * width + pair * 128, 128) for j in range(3)]
        query, key, value = joined[:, at[0]] * (64 ** -0.5), joined[:, at[1]] * (64 ** -0.5), joined[:, at[2]]
        grad_out = grad_mixed[:, at[0]]
        totals = [None] * 3
        for half in range(2):
            side = sides[half]
            prob = probs[2 * pair + half]
            grad_half = jnp.where(side, grad_out, 0).astype(BF)
            grad_prob = dot_nt(grad_half, value)
            wide = prob.astype(F32)
            mass = wide * grad_prob
            grad_score = (mass - wide * jnp.sum(mass, axis=-1, keepdims=True)).astype(BF)
            terms = (
                dot(grad_score, jnp.where(side, key, 0).astype(BF)),
                dot_tn(grad_score, jnp.where(side, query, 0).astype(BF)),
                dot_tn(prob, grad_half),
            )
            totals = [t if old is None else old + t for old, t in zip(totals, terms)]
        for j in range(3):
            grad_joined[:, at[j]] = totals[j].astype(BF)
    sums[2:3, :] = column_sum(grad_joined[:, pl.ds(0, width)].astype(F32))
    sums[3:4, :] = column_sum(grad_joined[:, pl.ds(2 * width, width)].astype(F32))
    grad_first[...] = dot_nt(grad_joined[...], attend_v[...])

    def emit(rows, result):
        grad_in[rows, :] = result
        low[rows, :] = result.astype(BF)

    sums[0:1, :], sums[1:2, :], _ = norm_back_all(
        grad_first, gains[0, 0:1, :], unit, factors, 0, lambda rows: grad_resid[rows, :], emit
    )


def only_where(section_ref, only, run):
    if only is None:
        run()
    else:
        pl.when(section_ref[0] == only)(run)


def outer_kernel(own, only, where_ref, gains, ends, incoming, *rest):
    unit_two, factors, slope, output_v, expand_v, reduce_v, *rest = rest
    *outs, g, grad_second, in_sem = rest
    outs = outs[-6:]

    def run():
        if only != 0:
            @pl.when(where_ref[0] != 0)
            def _():
                copy = pltpu.make_async_copy(ends.at[0, own], g, in_sem)
                copy.start()
                copy.wait()
        if only != 1:
            @pl.when(where_ref[0] == 0)
            def _():
                g[...] = incoming[...].astype(F32)

        backward_outer(
            gains, g, unit_two, factors, slope, output_v, expand_v, reduce_v, *outs, grad_second
        )

    only_where(where_ref, only, run)


def inner_kernel(only, where_ref, gains, grad_resid, grad_mixed, joined, probs, unit, factors, attend_v, *rest):
    *outs, grad_first = rest
    outs = outs[-4:]

    def run():
        backward_inner(
            gains, grad_resid, grad_mixed, joined, probs, unit, factors, attend_v, *outs, grad_first
        )

    only_where(where_ref, only, run)


def backward_one(own, only, where, gains, ends, incoming, slot, weights, saved=None):
    count, width = ends.shape[2:]
    hidden = slot[8].shape[1]
    shapes = [
        ((count, width), BF), ((count, hidden), BF), ((count, width), BF), ((count, width), F32),
        ((count, width), BF), ((8, width), F32),
    ]
    saved = [] if saved is None else [pinned(s) for s in saved]
    used = [slot[i] for i in (5, 6, 9)] + list(weights[1:])
    return pl.pallas_call(
        functools.partial(outer_kernel, own, only),
        out_shape=[pltpu.VMEM(*s) for s in shapes],
        in_specs=[SM, VM, HB] + [VM] * (7 + len(saved)),
        out_specs=[VM] * len(shapes),
        scratch_shapes=[pltpu.VMEM((count, width), F32), pltpu.VMEM((count, width), F32), pltpu.SemaphoreType.DMA],
        input_output_aliases={10 + i: i for i in range(len(saved))},
        compiler_params=pltpu.CompilerParams(vmem_limit_bytes=LIMIT),
        name="backward_outer",
    )(where, gains, in_hbm(ends), pinned(incoming), *[pinned(v) for v in used], *saved)


def backward_two(only, where, gains, outer, slot, weights, saved=None):
    count, width = outer[3].shape
    shapes = [((count, 3 * width), BF), ((count, width), F32), ((count, width), BF), ((8, width), F32)]
    saved = [] if saved is None else [pinned(s) for s in saved]
    used = [outer[3], outer[4]] + [slot[i] for i in (1, 2, 4, 6)] + [weights[0]]
    return pl.pallas_call(
        functools.partial(inner_kernel, only),
        out_shape=[pltpu.VMEM(*s) for s in shapes],
        in_specs=[SM, VM] + [VM] * (7 + len(saved)),
        out_specs=[VM] * len(shapes),
        scratch_shapes=[pltpu.VMEM((count, width), F32)],
        input_output_aliases={9 + i: i for i in range(len(saved))},
        compiler_params=pltpu.CompilerParams(vmem_limit_bytes=LIMIT),
        name="backward_inner",
    )(where, gains, *[pinned(v) for v in used], *saved)


def product_kernel(pieces, where_ref, *refs):
    *operands, keep, send = refs
    core = where_ref[4]
    pairs, own_rows, width = keep.shape
    group = 2 * own_rows
    per = pieces
    for start in range(0, pairs, per):
        cols = pl.ds(start * group, per * group)
        total = None
        for left, right in zip(operands[0::2], operands[1::2]):
            term = dot_tn(left[:, cols], right[...])
            total = term if total is None else total + term
        total = total.astype(BF).reshape(per, 2, own_rows, width)
        for j in range(per):
            keep[start + j] = jnp.where(core == 0, total[j, 0], total[j, 1])
            send[start + j] = jnp.where(core == 0, total[j, 1], total[j, 0])


def product(where, lefts, rights, devices, pieces, name):
    rows, width = lefts[0].shape[1], rights[0].shape[1]
    shape = (devices // 2, rows // devices, width)
    operands = [pinned(v) for pair in zip(lefts, rights) for v in pair]
    return pl.pallas_call(
        functools.partial(product_kernel, pieces),
        out_shape=[jax.ShapeDtypeStruct(shape, BF)] * 2,
        in_specs=[SM] + [VM] * len(operands),
        out_specs=[VM] * 2,
        compiler_params=pltpu.CompilerParams(vmem_limit_bytes=LIMIT),
        name=name,
    )(where, *operands)


def combine_kernel(bit, where_ref, keep, received, next_keep, next_send):
    mine = where_ref[bit]
    for i in range(next_keep.shape[0]):
        near, far = 2 * i + mine, 2 * i + 1 - mine
        next_keep[i] = (keep[near].astype(F32) + received[near].astype(F32)).astype(BF)
        next_send[i] = (keep[far].astype(F32) + received[far].astype(F32)).astype(BF)


def combine(bit, where, keep, received):
    shape = (keep.shape[0] // 2, *keep.shape[1:])
    return pl.pallas_call(
        functools.partial(combine_kernel, bit),
        out_shape=[jax.ShapeDtypeStruct(shape, BF)] * 2,
        in_specs=[SM, VM, VM],
        out_specs=[VM] * 2,
        compiler_params=pltpu.CompilerParams(vmem_limit_bytes=LIMIT),
        name="combine",
    )(where, keep, received)


def edge_kernel(where_ref, grad_zero, grad_one, out_zero, out_one, edges, sems):
    def run(parts):
        copies = [pltpu.make_async_copy(part, edges.at[0, i], sems.at[i]) for i, part in enumerate(parts)]
        for copy in copies:
            copy.start()
        for copy in copies:
            copy.wait()

    pl.when(where_ref[0] == 0)(lambda: run((grad_zero, grad_one)))
    pl.when(where_ref[0] != 0)(lambda: run((out_zero, out_one)))


def edges_of(where, parts):
    return pl.pallas_call(
        edge_kernel,
        out_shape=jax.ShapeDtypeStruct((1, 2, *parts[0].shape), F32),
        in_specs=[SM] + [VM] * 4,
        out_specs=HB,
        scratch_shapes=[pltpu.SemaphoreType.DMA((2,))],
        compiler_params=pltpu.CompilerParams(vmem_limit_bytes=LIMIT),
        name="edges",
    )(where, *[pinned(p) for p in parts])


def shifted(value, axis, by):
    devices = lax.axis_size(axis)
    pairs = [(i, i + by) for i in range(devices) if 0 <= i + by < devices]
    return lax.ppermute(value, axis, pairs)


def exchanged(value, axis, bit):
    return lax.ppermute(value, axis, [(i, i ^ bit) for i in range(lax.axis_size(axis))])


def scattered(where, keep, send, devices):
    level = 1
    while True:
        received = exchanged(send, "dp", level)
        if keep.shape[0] == 1:
            return keep[0].astype(F32) + received[0].astype(F32)
        keep, send = combine(4 + level.bit_length(), where, keep, received)
        level *= 2


def shards(
    ends, lengths, norm_gains, norm_shifts, attend_weight, offsets, output_weight, expand_weight, expand_bias, reduce_weight
):
    section, place = lax.axis_index("section"), lax.axis_index("dp")
    devices = lax.axis_size("dp")
    levels = devices.bit_length() - 1
    width = ends.shape[3]
    hidden = expand_weight.shape[2]
    zero = jnp.zeros_like(section)
    where = jnp.stack(
        [section, zero, 1 - section, zero + 1] + [(place >> i) & 1 for i in range(levels)]
    ).astype(jnp.int32)
    small = (norm_gains, norm_shifts, offsets, expand_bias)
    weights = (attend_weight, output_weight, expand_weight, reduce_weight)

    slot_a, held = forward_first(where, lengths, small, ends, weights)
    incoming = shifted(slot_a[11], "section", 1)
    slot_b = forward_later(1, where, lengths, small, ends, incoming, held)
    later = shifted(slot_b[11], "section", 1)
    outer_b = backward_one(0, 1, where, norm_gains, ends, incoming, slot_b, held)
    inner_b = backward_two(1, where, norm_gains, outer_b, slot_b, held)
    grad_zero = shifted(inner_b[2], "section", -1)
    slot_a = forward_later(2, where, lengths, small, ends, later, held, slot_a)
    outer_a = backward_one(1, None, where, norm_gains, ends, grad_zero, slot_a, held)
    inner_a = backward_two(None, where, norm_gains, outer_a, slot_a, held)
    grad_one = shifted(inner_a[2], "section", -1)
    outer_low = outer_b[0]
    g_low = jnp.where(section == 0, grad_one, outer_low)
    outer_b = backward_one(1, 0, where, norm_gains, ends, grad_one, slot_b, held, outer_b)
    inner_b = backward_two(0, where, norm_gains, outer_b, slot_b, held, inner_b)
    sums_outer, sums_inner = outer_a[5] + outer_b[5], inner_a[3] + inner_b[3]
    edges = edges_of(where, (inner_a[1], inner_b[1], slot_b[10], slot_a[10]))

    operands = {
        "reduce": ([outer_a[0], g_low], [slot_a[8], slot_b[8]], 4),
        "expand": ([outer_a[1], outer_b[1]], [slot_a[7], slot_b[7]], 1),
        "attend": ([inner_a[0], inner_b[0]], [slot_a[0], slot_b[0]], 2),
        "output": ([outer_a[2], outer_b[2]], [slot_a[3], slot_b[3]], 4),
    }
    aligned = devices == 2 ** levels and devices > 1 and (width // devices) % 16 == 0
    grads = {}
    for name, (lefts, rights, pieces) in operands.items():
        if aligned:
            keep, send = product(where, lefts, rights, devices, pieces, name)
            grads[name] = scattered(where, keep, send, devices).T[None]
        else:
            term = sum(dot_tn(right, left) for left, right in zip(lefts, rights)).astype(BF)
            grads[name] = lax.psum_scatter(term, "dp", scatter_dimension=1, tiled=True).astype(F32)[None]
    rows = jnp.concatenate([sums_inner[0:1], sums_outer[0:1], sums_inner[1:2], sums_outer[1:2], sums_inner[2:4], sums_outer[2:4]])
    share = width // devices
    rows = jnp.swapaxes(rows.reshape(8, devices, share), 0, 1).reshape(devices, 8 * share)
    bias = sums_outer[4 : 4 + hidden // width].reshape(devices, hidden // devices)
    little = lax.psum_scatter(jnp.concatenate([rows, bias], axis=1), "dp", scatter_dimension=0, tiled=True)
    rows = little[0, : 8 * share].reshape(8, share)
    return (
        edges,
        rows[0:2][None],
        rows[2:4][None],
        grads["attend"],
        rows[4:8][None],
        grads["output"],
        grads["expand"],
        little[:, 8 * share :],
        grads["reduce"],
    )


def solution(mesh):
    in_specs = (
        P("section", None, "dp", None),
        P(None, "dp", None),
        P("section", None, None),
        P("section", None, None),
        P("section", None, None),
        P("section", None, None),
        P("section", None, None),
        P("section", None, None),
        P("section", None),
        P("section", None, None),
    )
    out_specs = (
        P("section", None, "dp", None),
        P("section", None, "dp"),
        P("section", None, "dp"),
        P("section", None, "dp"),
        P("section", None, "dp"),
        P("section", None, "dp"),
        P("section", None, "dp"),
        P("section", "dp"),
        P("section", None, "dp"),
    )
    return jax.shard_map(shards, mesh=mesh, in_specs=in_specs, out_specs=out_specs, check_vma=False)
```

```python
import functools

import jax
import jax.numpy as jnp
from jax import lax
from jax.experimental import pallas as pl
from jax.experimental.pallas import tpu as pltpu
from jax.sharding import PartitionSpec as P

HEADS = 12
ROWS = 32
LIMIT = 7 * 2**20
BF = jnp.bfloat16
F32 = jnp.float32
VM = pl.BlockSpec(memory_space=pltpu.VMEM)
HB = pl.BlockSpec(memory_space=pltpu.HBM)


def in_hbm(value):
    return pltpu.with_memory_space_constraint(value, pltpu.HBM)


def pinned(value):
    return pltpu.with_memory_space_constraint(value, pltpu.VMEM)


def dot(left, right, dims=((1,), (0,))):
    return lax.dot_general(left, right, (dims, ((), ())), preferred_element_type=F32)


def dot_nt(left, right):
    return dot(left, right, ((1,), (1,)))


def dot_tn(left, right):
    return dot(left, right, ((0,), (0,)))


class Layout:
    def __init__(self, count, width, hidden):
        self.count, self.width, self.hidden = count, width, hidden
        self.place, self.size = {}, [0, 0, 0, 0]
        self.lanes = (width, 3 * width, hidden, width)
        self.put(0, "output_w", width)
        self.put(0, "reduce_w", hidden)
        for name in ("first", "mixed", "second", "g_low", "resid_low"):
            self.put(0, name + "0", count)
            self.put(0, name + "1", count)
        self.put(0, "grad_mixed", count)
        self.put(1, "attend_w", width)
        for name in ("joined0", "joined1", "grad_joined0", "grad_joined1"):
            self.put(1, name, count)
        self.put(2, "expand_w", width)
        for name in ("slope0", "probs0", "slope1", "probs1", "act0", "act1", "pre_low0", "pre_low1"):
            self.put(2, name, count)
        for name in ("unit0", "unit1", "unit_two0", "unit_two1", "edge0", "edge1", "grad_resid", "mixture"):
            self.put(3, name, count)
        self.put(3, "params", 16)
        self.put(3, "sums0", 16)
        self.put(3, "sums1", 16)
        for name, old, offset in (("reduce", "slope0", 0), ("expand", "reduce_w", 0), ("attend", "reduce_w", hidden // 2), ("output", "output_w", 0)):
            arena, start, _ = self.place[old]
            self.place["keep_" + name] = (arena, start + offset, 0)

    def put(self, arena, name, rows):
        self.place[name] = (arena, self.size[arena], rows)
        self.size[arena] += rows

    def shapes(self):
        return [pltpu.VMEM((rows, lanes), F32 if i == 3 else BF) for i, (rows, lanes) in enumerate(zip(self.size, self.lanes))]

    def views(self, arenas, slot=None):
        def view(name):
            arena, start, rows = self.place[name if name in self.place else name + str(slot)]
            return arenas[arena].at[pl.ds(start, rows), :]

        return view

    def cut(self, arenas, name):
        arena, start, rows = self.place[name]
        return arenas[arena][start : start + rows]


def run(body, arenas, layout, ins=(), in_specs=(), outs=(), out_specs=(), scratch=(), name=None, micros=1, aliases=None):
    held = [] if arenas is None else [pinned(arena) for arena in arenas]
    given, kept = len(held) + len(ins), len(layout.lanes)

    def kernel(*refs):
        body(refs[given : given + kept], *refs[len(held) : given], *refs[given + kept :])

    result = pl.pallas_call(
        kernel,
        out_shape=layout.shapes() + list(outs),
        in_specs=[VM] * len(held) + list(in_specs),
        out_specs=[VM] * kept + list(out_specs),
        scratch_shapes=list(scratch),
        input_output_aliases={
            **{i: i for i in range(len(held))}, **{len(held) + i: kept + o for i, o in (aliases or {}).items()}
        },
        compiler_params=pltpu.CompilerParams(vmem_limit_bytes=LIMIT),
        cost_estimate=pl.CostEstimate(flops=int(micros * 1e9), bytes_accessed=0, transcendentals=0),
        name=name,
    )(*held, *ins)
    return list(result[:kept]), list(result[kept:])


def group_bias(lengths_ref, micro, count):
    rows = lax.broadcasted_iota(jnp.int32, (count, count), 0)
    cols = lax.broadcasted_iota(jnp.int32, (count, count), 1)
    bound = jnp.int32(0)
    row_group = jnp.zeros((count, count), jnp.int32)
    col_group = jnp.zeros((count, count), jnp.int32)
    for crop in range(lengths_ref.shape[2]):
        bound = bound + lengths_ref[micro, 0, crop]
        row_group = row_group + (rows >= bound).astype(jnp.int32)
        col_group = col_group + (cols >= bound).astype(jnp.int32)
    return jnp.where(row_group == col_group, 0.0, -1e30).astype(F32)


def gelu_parts(pre):
    size = jnp.abs(pre) * (2.0 ** -0.5)
    bell = jnp.exp(-size * size)
    t = 1.0 / (1.0 + 0.3275911 * size)
    poly = t * (0.254829592 + t * (-0.284496736 + t * (1.421413741 + t * (-1.453152027 + t * 1.061405429))))
    tail = 0.5 * poly * bell
    upper = jnp.where(pre >= 0, 1.0 - tail, tail)
    return pre * upper, upper + pre * (bell * 0.3989422804014327)


def norm_rows(values):
    center = values - jnp.mean(values, axis=-1, keepdims=True)
    factor = lax.rsqrt(jnp.mean(center * center, axis=-1, keepdims=True) + 1e-06)
    return center * factor, factor


def halves(count):
    lane = lax.broadcasted_iota(jnp.int32, (count, 128), 1)
    return lane < 64, lane >= 64


def factor_column(count, slot, norm):
    column = 2 * count + 128 * slot + norm
    return slice(column, column + 1)


def forward_body(view, slot, micro, a, low, ready):
    count, width = a.shape
    first, joined, probs, mixed, act, slope = (view(n) for n in ("first", "joined", "probs", "mixed", "act", "slope"))
    unit, unit_two, out, second, mixture, params = (view(n) for n in ("unit", "unit_two", "edge", "second", "mixture", "params"))
    attend_w, output_w, expand_w, reduce_w = (view(n) for n in ("attend_w", "output_w", "expand_w", "reduce_w"))
    hidden = act.shape[1]
    bias = pl.ds(pl.multiple_of(micro * count, 128), count)

    def norm(source, unit, target, index):
        gain, shift = params[index : index + 1, :], params[2 + index : 3 + index, :]
        for r in range(0, count, ROWS):
            rows = pl.ds(r, ROWS)
            normed, factor = norm_rows(source[rows, :])
            unit[rows, :] = normed
            mixture[rows, factor_column(count, slot, index)] = factor
            target[rows, :] = (normed * gain + shift).astype(BF)

    norm(a, unit, first, 0)
    for i in range(3):
        ready("attend_w", i)
        cols = pl.ds(i * width, width)
        part = dot(first[...], attend_w[:, cols])
        if i == 0:
            part = part + params[4:5, :]
        if i == 2:
            part = part + params[5:6, :]
        joined[:, cols] = part.astype(BF)

    sides = halves(count)
    for pair in range(HEADS // 2):
        query = joined[:, pl.ds(pair * 128, 128)] * (64 ** -0.5)
        key = joined[:, pl.ds(width + pair * 128, 128)]
        value = joined[:, pl.ds(2 * width + pair * 128, 128)]
        total = None
        for half in range(2):
            scores = dot_nt(jnp.where(sides[half], query, 0).astype(BF), key) + mixture[:, bias]
            weights = jnp.exp(scores - jnp.max(scores, axis=-1, keepdims=True))
            prob = (weights * (1.0 / jnp.sum(weights, axis=-1, keepdims=True))).astype(BF)
            probs[:, pl.ds((2 * pair + half) * count, count)] = prob
            term = dot(prob, jnp.where(sides[half], value, 0).astype(BF))
            total = term if total is None else total + term
        mixed[:, pl.ds(pair * 128, 128)] = total.astype(BF)

    ready("output_w", 0)
    out[...] = a[...] + dot(mixed[...], output_w[...]) + params[6:7, :]
    norm(out, unit_two, second, 1)
    for i in range(hidden // width):
        cols = pl.ds(i * width, width)
        ready("expand_w", i)
        pre = dot(second[...], expand_w[:, cols]) + params[8 + i : 9 + i, :]
        value, grad = gelu_parts(pre)
        act[:, cols] = value.astype(BF)
        slope[:, cols] = grad.astype(BF)
        ready("reduce_w", i)
        out[...] += dot(act[:, cols], reduce_w[cols, :])
    out[...] += params[7:8, :]
    low[...] = out[...].astype(BF)


def forward_first(layout, ends, lengths, small, weights):
    count, width, hidden = layout.count, layout.width, layout.hidden
    tiles = hidden // width

    def body(arenas, ends, lengths, gains, shifts, offsets, bias, attend, output, expand, reduce, low, *scratch):
        a, lengths_s, gains_v, shifts_v, offsets_v, bias_v, sems, first_sems = scratch
        view = layout.views(arenas, 0)
        params, mixture = view("params"), view("mixture")
        attend_w, output_w, expand_w, reduce_w = (view(n) for n in ("attend_w", "output_w", "expand_w", "reduce_w"))
        early = [
            pltpu.make_async_copy(source, target, first_sems.at[i])
            for i, (source, target) in enumerate(
                [
                    (lengths, lengths_s), (ends.at[0, 0], a), (gains, gains_v), (shifts, shifts_v),
                    (offsets, offsets_v), (bias, bias_v),
                ]
            )
        ]
        for copy in early:
            copy.start()
        copies = {}
        for i in range(3):
            cols = pl.ds(i * width, width)
            copies["attend_w", i] = attend.at[0, :, cols], attend_w.at[:, cols]
        copies["output_w", 0] = output.at[0], output_w
        for i in range(tiles):
            cols = pl.ds(i * width, width)
            copies["expand_w", i] = expand.at[0, :, cols], expand_w.at[:, cols]
            copies["reduce_w", i] = reduce.at[0, cols], reduce_w.at[cols, :]
        order = list(copies)
        for number, name in enumerate(order):
            copies[name] = pltpu.make_async_copy(*copies[name], sems.at[number])
        for name in order[:4]:
            copies[name].start()
        for copy in early:
            copy.wait()
        params[0:2, :] = gains_v[0]
        params[2:4, :] = shifts_v[0]
        params[4:8, :] = offsets_v[0]
        for i in range(tiles):
            params[8 + i : 9 + i, :] = bias_v[0:1, pl.ds(i * width, width)]
        for micro in range(lengths.shape[0]):
            mixture[:, pl.ds(micro * count, count)] = group_bias(lengths_s, micro, count)

        def ready(name, i):
            copies[name, i].wait()
            if (name, i) == ("attend_w", 2):
                for later in order[4:]:
                    copies[later].start()

        section = lax.axis_index("section")
        pl.when(section == 0)(lambda: forward_body(view, 0, 0, a, low, ready))

        @pl.when(section != 0)
        def _():
            for name in order:
                ready(*name)

    return run(
        body, None, layout,
        ins=[in_hbm(v) for v in (ends, lengths, *small, *weights)], in_specs=[HB] * 10,
        outs=[pltpu.VMEM((count, width), BF)], out_specs=[VM],
        scratch=[
            pltpu.VMEM((count, width), F32), pltpu.SMEM(lengths.shape, jnp.int32),
            *[pltpu.VMEM(v.shape, F32) for v in small],
            pltpu.SemaphoreType.DMA((4 + 2 * tiles,)), pltpu.SemaphoreType.DMA((6,)),
        ],
        name="forward_first", micros=13,
    )


def forward_later(layout, arenas, slot, own, ends, incoming):
    count, width = layout.count, layout.width

    def body(arenas, ends, incoming, low, a, sem):
        view = layout.views(arenas, slot)
        section = lax.axis_index("section")

        def step(micro):
            forward_body(view, slot, micro, a, low, lambda name, i: None)

        if own is None:
            @pl.when(section != 0)
            def _():
                a[...] = incoming[...].astype(F32)
                step(ends.shape[1] - 1)

            return

        @pl.when(section == 0)
        def _():
            copy = pltpu.make_async_copy(ends.at[0, own], a, sem)
            copy.start()
            copy.wait()

        @pl.when(section != 0)
        def _():
            a[...] = incoming[...].astype(F32)

        step(own - section)

    return run(
        body, arenas, layout, ins=[in_hbm(ends), pinned(incoming)], in_specs=[HB, VM],
        outs=[pltpu.VMEM((count, width), BF)], out_specs=[VM],
        scratch=[pltpu.VMEM((count, width), F32), pltpu.SemaphoreType.DMA], name="forward_later", micros=11,
    )


def norm_back_all(grad, gain, normed_ref, factors, base, emit):
    count, width = normed_ref.shape
    sums = [jnp.zeros((8, width), F32)] * 3

    def fold(values):
        return jnp.sum(values.reshape(-1, 8, width), axis=0)

    for r in range(0, count, ROWS):
        rows = pl.ds(r, ROWS)
        part, normed = grad[rows, :], normed_ref[rows, :]
        scaled = part * gain
        result = base(rows) + factors(rows) * (
            scaled
            - jnp.mean(scaled, axis=-1, keepdims=True)
            - normed * jnp.mean(scaled * normed, axis=-1, keepdims=True)
        )
        sums = [total + fold(term) for total, term in zip(sums, (part * normed, part, result))]
        emit(rows, result)
    return [column_sum(total) for total in sums]


def column_sum(values):
    return jnp.sum(values, axis=0, keepdims=True)


def outer_body(view, slot, g, grad_second):
    count, width = g.shape
    slope, pre_low, g_low, resid_low, sums = (view(n) for n in ("slope", "pre_low", "g_low", "resid_low", "sums"))
    grad_resid, mixture, params = view("grad_resid"), view("mixture"), view("params")
    output_w, expand_w, reduce_w = view("output_w"), view("expand_w"), view("reduce_w")
    hidden = slope.shape[1]
    g_low[...] = g[...].astype(BF)
    sums[7:8, :] = column_sum(g[...])
    for i in range(hidden // width):
        cols = pl.ds(i * width, width)
        grad_pre = dot_nt(g_low[...], reduce_w[cols, :]) * slope[:, cols].astype(F32)
        sums[8 + i : 9 + i, :] = column_sum(grad_pre)
        pre_low[:, cols] = grad_pre.astype(BF)
        term = dot_nt(pre_low[:, cols], expand_w[:, cols])
        if i == 0:
            grad_second[...] = term
        else:
            grad_second[...] += term

    def emit(rows, result):
        grad_resid[rows, :] = result
        resid_low[rows, :] = result.astype(BF)

    sums[1:2, :], sums[3:4, :], sums[6:7, :] = norm_back_all(
        grad_second, params[1:2, :], view("unit_two"), lambda rows: mixture[rows, factor_column(count, slot, 1)],
        lambda rows: g[rows, :], emit,
    )
    view("grad_mixed")[...] = dot_nt(resid_low[...], output_w[...]).astype(BF)


def inner_body(view, slot, low, grad_first):
    grad_resid, grad_mixed, joined, probs = view("grad_resid"), view("grad_mixed"), view("joined"), view("probs")
    grad_joined, edge, sums = view("grad_joined"), view("edge"), view("sums")
    first_layer = lax.axis_index("section") == 0
    mixture, params, attend_w = view("mixture"), view("params"), view("attend_w")
    count, width = grad_resid.shape
    sides = halves(count)
    for pair in range(HEADS // 2):
        at = [pl.ds(j * width + pair * 128, 128) for j in range(3)]
        query, key, value = joined[:, at[0]] * (64 ** -0.5), joined[:, at[1]] * (64 ** -0.5), joined[:, at[2]]
        grad_out = grad_mixed[:, at[0]]
        totals = [None] * 3
        for half in range(2):
            side = sides[half]
            prob = probs[:, pl.ds((2 * pair + half) * count, count)]
            grad_half = jnp.where(side, grad_out, 0).astype(BF)
            grad_prob = dot_nt(grad_half, value)
            wide = prob.astype(F32)
            mass = wide * grad_prob
            grad_score = (mass - wide * jnp.sum(mass, axis=-1, keepdims=True)).astype(BF)
            terms = (
                dot(grad_score, jnp.where(side, key, 0).astype(BF)),
                dot_tn(grad_score, jnp.where(side, query, 0).astype(BF)),
                dot_tn(prob, grad_half),
            )
            totals = [t if old is None else old + t for old, t in zip(totals, terms)]
        for j in range(3):
            grad_joined[:, at[j]] = totals[j].astype(BF)
    sums[4:5, :] = column_sum(grad_joined[:, pl.ds(0, width)].astype(F32))
    sums[5:6, :] = column_sum(grad_joined[:, pl.ds(2 * width, width)].astype(F32))
    grad_first[...] = dot_nt(grad_joined[...], attend_w[...])

    def emit(rows, result):
        edge[rows, :] = jnp.where(first_layer, result, edge[rows, :])
        low[rows, :] = result.astype(BF)

    sums[0:1, :], sums[2:3, :], _ = norm_back_all(
        grad_first, params[0:1, :], view("unit"), lambda rows: mixture[rows, factor_column(count, slot, 0)],
        lambda rows: grad_resid[rows, :], emit,
    )


def only_on(only, step):
    if only is None:
        step()
    else:
        pl.when(lax.axis_index("section") == only)(step)


def backward_outer(layout, arenas, slot, own, only, ends, incoming):
    count, width = layout.count, layout.width

    def body(arenas, ends, incoming, g, grad_second, sem):
        view = layout.views(arenas, slot)
        section = lax.axis_index("section")

        def step():
            if only != 0:
                @pl.when(section != 0)
                def _():
                    copy = pltpu.make_async_copy(ends.at[0, own], g, sem)
                    copy.start()
                    copy.wait()
            if only != 1:
                @pl.when(section == 0)
                def _():
                    g[...] = incoming[...].astype(F32)
            outer_body(view, slot, g, grad_second)

        only_on(only, step)

    return run(
        body, arenas, layout, ins=[in_hbm(ends), pinned(incoming)], in_specs=[HB, VM],
        scratch=[pltpu.VMEM((count, width), F32), pltpu.VMEM((count, width), F32), pltpu.SemaphoreType.DMA],
        name="backward_outer", micros=5,
    )[0]


def backward_inner(layout, arenas, slot, only, last=False):
    count, width = layout.count, layout.width
    outs, out_specs, scratch = end_outputs(layout) if last else ([], [], [])

    def body(arenas, low, *refs):
        *refs, grad_first = refs
        only_on(only, lambda: inner_body(layout.views(arenas, slot), slot, low, grad_first))
        if last:
            write_ends(layout, arenas, *refs)

    return run(
        body, arenas, layout, outs=[pltpu.VMEM((count, width), BF), *outs], out_specs=[VM, *out_specs],
        scratch=[*scratch, pltpu.VMEM((count, width), F32)], name="backward_inner", micros=6,
    )


FACTORS = {
    "reduce": ("g_low", "act", 8), "expand": ("pre_low", "second", 2), "attend": ("grad_joined", "first", 4),
    "output": ("resid_low", "mixed", 8),
}


def spread(sums, place, devices, hidden):
    width = sums.shape[1]
    share, wide = width // devices, hidden // devices
    bias = 8 + place * wide // width
    rows = (sums[:8], jnp.broadcast_to(sums[bias : bias + 1], (8, width)))
    starts = (place * share, place * wide % width)
    return jnp.concatenate([pltpu.roll(row, (width - start) % width, 1) for row, start in zip(rows, starts)])


class Share:
    def __init__(self, layout, devices, name, part, parts, order, extra=False):
        left, right, self.per = FACTORS[name]
        self.layout, self.name, self.left, self.right, self.extra = layout, name, left, right, extra
        self.own = layout.lanes[layout.place[left + "0"][0]] // devices
        self.rows = self.own + (16 if extra else 0)
        self.columns = layout.lanes[layout.place[right + "0"][0]] // parts
        self.lanes = pl.ds(part * self.columns, self.columns)
        self.pairs, self.parts, self.whole = devices // 2, parts, parts == 1
        self.todo, self.free = list(order), list(range(self.pairs.bit_length() - 1))
        arena, start, _ = layout.place["keep_" + name]
        room_lanes = self.lanes if name == "reduce" else slice(None)

        def block(arenas, pair):
            row = start + pair * self.rows
            return arenas[arena].at[pl.ds(row if isinstance(row, int) else pl.multiple_of(row, 16), self.rows), room_lanes]

        self.block = block

    def make(self, arenas, incoming=None):
        ins = [] if incoming is None else [incoming]

        def body(arenas, *refs):
            *given, send = refs
            core = lax.rem(lax.axis_index("dp"), 2)
            if incoming is not None:
                @pl.when(lax.axis_index("section") == 0)
                def _():
                    self.layout.views(arenas)("g_low1")[...] = given[0][...]

            if self.extra:
                view = self.layout.views(arenas)
                sums = view("sums0")[...] + view("sums1")[...]
                for pair in range(self.pairs):
                    low, high = (spread(sums, 2 * pair + half, 2 * self.pairs, self.layout.hidden) for half in range(2))
                    for target, half in ((self.block(arenas, pair), core), (send.at[pair], 1 - core)):
                        target[self.own :, :] = jnp.where(half == 0, low, high).astype(BF)

            per = min(self.per, self.pairs)
            for start in range(0, self.pairs, per):
                rows = pl.ds(2 * start * self.own, 2 * per * self.own)
                total = None
                for slot in range(2):
                    view = self.layout.views(arenas, slot)
                    term = dot_tn(view(self.left)[:, rows], view(self.right)[:, self.lanes])
                    total = term if total is None else total + term
                total = total.astype(BF).reshape(per, 2, self.own, self.columns)
                for j in range(per):
                    self.block(arenas, start + j)[: self.own, :] = jnp.where(core == 0, total[j, 0], total[j, 1])
                    send[start + j, : self.own, :] = jnp.where(core == 0, total[j, 1], total[j, 0])

        arenas, (send,) = run(
            body, arenas, self.layout, ins=[pinned(v) for v in ins], in_specs=[VM] * len(ins),
            outs=[pltpu.VMEM((self.pairs, self.rows, self.columns), BF)], out_specs=[VM], name=self.name, micros=2,
        )
        self.moved = exchanged(send, 1)
        return arenas

    def step(self, arenas, result=None):
        free, done = list(self.free), [place for place in range(self.pairs.bit_length() - 1) if place not in self.free]
        bit = self.todo.pop(0) if self.todo else None
        place = None if bit is None else bit.bit_length() - 2
        rest = [p for p in free if p != place]
        self.earlier = result is not None

        def body(arenas, moved, *refs):
            device = lax.axis_index("dp")

            def mine(place):
                return lax.rem(lax.div(device, 2 << place), 2)

            base = sum((mine(p) << p for p in done), 0)

            def spot(number, side):
                bits = {p: (number >> k) & 1 for k, p in enumerate(rest)}
                if place is not None:
                    bits[place] = side
                index = sum((bits[p] << k for k, p in enumerate(free)), 0)
                return base + sum((bits[p] << p for p in free), 0), index

            if place is None:
                pair, index = spot(0, None)
                self.finish(self.block(arenas, pair)[...].astype(F32) + moved[index].astype(F32), *refs)
                return
            target, side = refs[0], mine(place)
            for number in range(1 << len(rest)):
                pair, index = spot(number, 1 - side)
                target[number] = self.block(arenas, pair)[...] + moved[index]
                pair, index = spot(number, side)
                block = self.block(arenas, pair)
                block[...] = block[...] + moved[index]

        outs, out_specs, scratch, ins = self.targets(result) if place is None else (
            [pltpu.VMEM((1 << len(rest), self.rows, self.columns), BF)], [VM], [], []
        )
        arenas, results = run(
            body, arenas, self.layout, ins=[pinned(self.moved), *ins], in_specs=[VM] + [HB] * len(ins), outs=outs,
            out_specs=out_specs, scratch=scratch, name="add_" + self.name, aliases={1: 0} if ins else {},
        )
        if place is None:
            return arenas, results
        self.moved = exchanged(results[0], bit)
        self.free = rest
        return arenas

    def targets(self, result):
        width, hidden, devices = self.layout.width, self.layout.hidden, 2 * self.pairs
        share = width // devices
        full = self.columns if self.whole else self.lanes.size * self.parts
        outs, specs = [jax.ShapeDtypeStruct((self.own, full), F32)], [HB]
        if self.extra:
            outs += [jax.ShapeDtypeStruct((1, n, share), F32) for n in (2, 2, 4)]
            outs += [jax.ShapeDtypeStruct((1, hidden // devices), F32)]
            specs += [VM] * 4
        scratch = [pltpu.VMEM((self.own, self.columns), F32), pltpu.SemaphoreType.DMA]
        return outs, specs, scratch, [] if result is None else [in_hbm(result)]

    def finish(self, total, *refs):
        *refs, held, sem = refs
        if self.earlier:
            refs = refs[1:]
        held[...] = total[: self.own]
        lanes = pl.ds(0, self.columns) if self.whole else self.lanes
        copy = pltpu.make_async_copy(held, refs[0].at[:, lanes], sem)
        copy.start()
        if self.extra:
            small, start = total[self.own :], 0
            for target in refs[1:4]:
                count, share = target.shape[1:]
                target[0] = small[start : start + count, :share]
                start += count
            refs[4][...] = small[8:9, : refs[4].shape[1]]
        copy.wait()


def end_outputs(layout):
    return [jax.ShapeDtypeStruct((1, 2, layout.count, layout.width), F32)], [HB], [pltpu.SemaphoreType.DMA((2,))]


def write_ends(layout, arenas, edges, sems):
    view = layout.views(arenas)

    def move(names):
        copies = [pltpu.make_async_copy(view(name), edges.at[0, i], sems.at[i]) for i, name in enumerate(names)]
        for copy in copies:
            copy.start()
        for copy in copies:
            copy.wait()

    section = lax.axis_index("section")
    pl.when(section == 0)(lambda: move(("edge0", "edge1")))
    pl.when(section != 0)(lambda: move(("edge1", "edge0")))


def shifted(value, axis, by):
    devices = lax.axis_size(axis)
    pairs = [(i, i + by) for i in range(devices) if 0 <= i + by < devices]
    return lax.ppermute(value, axis, pairs)


def exchanged(value, bit):
    return lax.ppermute(value, "dp", [(i, i ^ bit) for i in range(lax.axis_size("dp"))])


def shards(
    ends, lengths, norm_gains, norm_shifts, attend_weight, offsets, output_weight, expand_weight, expand_bias, reduce_weight
):
    devices = lax.axis_size("dp")
    count, width = ends.shape[2:]
    hidden = expand_weight.shape[2]
    layout = Layout(count, width, hidden)
    small = (norm_gains, norm_shifts, offsets, expand_bias)
    weights = (attend_weight, output_weight, expand_weight, reduce_weight)

    arenas, (low,) = forward_first(layout, ends, lengths, small, weights)
    incoming = shifted(low, "section", 1)
    arenas, (low,) = forward_later(layout, arenas, 1, 1, ends, incoming)
    later = shifted(low, "section", 1)
    arenas = backward_outer(layout, arenas, 1, 0, 1, ends, incoming)
    arenas, (low,) = backward_inner(layout, arenas, 1, 1)
    grad_zero = shifted(low, "section", -1)
    arenas, _ = forward_later(layout, arenas, 0, None, ends, later)
    arenas = backward_outer(layout, arenas, 0, 1, None, ends, grad_zero)
    arenas, (low,) = backward_inner(layout, arenas, 0, None)
    grad_one = shifted(low, "section", -1)
    aligned = devices > 1 and devices & (devices - 1) == 0 and (width // devices) % 16 == 0
    grads = {}
    if aligned:
        up = [2**i for i in range(1, devices.bit_length() - 1)]
        side = up[1:] + up[:1]
        r0 = Share(layout, devices, "reduce", 0, 2, up)
        r1 = Share(layout, devices, "reduce", 1, 2, side)
        ex = Share(layout, devices, "expand", 0, 1, up)
        at = Share(layout, devices, "attend", 0, 1, up, True)
        ou = Share(layout, devices, "output", 0, 1, side)
        arenas = r0.make(arenas, grad_one)
        arenas = r1.make(arenas)
        arenas = r0.step(arenas)
        arenas = r1.step(arenas)
        arenas = backward_outer(layout, arenas, 1, 1, 0, ends, grad_one)
        arenas = ex.make(arenas)
        arenas = ou.make(arenas)
        for part in (r0, r1, ex):
            arenas = part.step(arenas)
        arenas, (_, edges) = backward_inner(layout, arenas, 1, 0, True)
        arenas = ou.step(arenas)
        arenas = at.make(arenas)
        for part in (r0, r1, ou, at, ex):
            arenas = part.step(arenas)
        arenas, (reduce_grad,) = r0.step(arenas)
        arenas = ou.step(arenas)
        arenas, (reduce_grad,) = r1.step(arenas, reduce_grad)
        arenas = ex.step(arenas)
        arenas, (output_grad,) = ou.step(arenas)
        arenas = at.step(arenas)
        arenas, (expand_grad,) = ex.step(arenas)
        arenas = at.step(arenas)
        arenas, (attend_grad, gains, shifts, offset_grads, bias) = at.step(arenas)
        grads = {"reduce": reduce_grad.T[None], "expand": expand_grad.T[None], "attend": attend_grad.T[None], "output": output_grad.T[None]}
    else:
        arenas = backward_outer(layout, arenas, 1, 1, 0, ends, grad_one)
        arenas, (_, edges) = backward_inner(layout, arenas, 1, 0, True)
        sums = layout.cut(arenas, "sums0") + layout.cut(arenas, "sums1")
        for name, (left, right, _) in FACTORS.items():
            term = sum(dot_tn(layout.cut(arenas, right + s), layout.cut(arenas, left + s)) for s in "01").astype(BF)
            grads[name] = lax.psum_scatter(term, "dp", scatter_dimension=1, tiled=True).astype(F32)[None]
        bias = sums[8 : 8 + hidden // width].reshape(width, hidden // width)
        little = lax.psum_scatter(jnp.concatenate([sums[:8].T, bias], axis=1), "dp", scatter_dimension=0, tiled=True)
        gains, shifts, offset_grads = (little[:, i:j].T[None] for i, j in ((0, 2), (2, 4), (4, 8)))
        bias = little[:, 8:].reshape(1, -1)
    return (
        edges,
        gains,
        shifts,
        grads["attend"],
        offset_grads,
        grads["output"],
        grads["expand"],
        bias,
        grads["reduce"],
    )


def solution(mesh):
    in_specs = (
        P("section", None, "dp", None),
        P(None, "dp", None),
        P("section", None, None),
        P("section", None, None),
        P("section", None, None),
        P("section", None, None),
        P("section", None, None),
        P("section", None, None),
        P("section", None),
        P("section", None, None),
    )
    out_specs = (
        P("section", None, "dp", None),
        P("section", None, "dp"),
        P("section", None, "dp"),
        P("section", None, "dp"),
        P("section", None, "dp"),
        P("section", None, "dp"),
        P("section", None, "dp"),
        P("section", "dp"),
        P("section", None, "dp"),
    )
    return jax.shard_map(shards, mesh=mesh, in_specs=in_specs, out_specs=out_specs, check_vma=False)
```

```python
import jax
import jax.numpy as jnp
from jax import lax
from jax.experimental import pallas as pl
from jax.experimental.pallas import tpu as pltpu
from jax.sharding import PartitionSpec as P

HEADS = 12
STAGE = 0
ROWS = 32
LIMIT = 7 * 2**20
BF = jnp.bfloat16
F32 = jnp.float32
VM = pl.BlockSpec(memory_space=pltpu.VMEM)
HB = pl.BlockSpec(memory_space=pltpu.HBM)

SLOTTED = (
    FIRST, MIXED, SECOND, G_LOW, RESID_LOW, JOINED, GRAD_JOINED, SLOPE, PROBS, ACT, PRE_LOW, UNIT, UNIT_TWO, EDGE, SUMS
) = range(15)
SHARED = OUTPUT_W, REDUCE_W, GRAD_MIXED, ATTEND_W, EXPAND_W, GRAD_RESID, MIXTURE, PARAMS = range(15, 23)
REDUCE, EXPAND, ATTEND, OUTPUT = range(4)


def in_hbm(value):
    return pltpu.with_memory_space_constraint(value, pltpu.HBM)


def pinned(value):
    return pltpu.with_memory_space_constraint(value, pltpu.VMEM)


def dot(left, right, dims=((1,), (0,))):
    return lax.dot_general(left, right, (dims, ((), ())), preferred_element_type=F32)


def dot_nt(left, right):
    return dot(left, right, ((1,), (1,)))


def dot_tn(left, right):
    return dot(left, right, ((0,), (0,)))


class Layout:
    def __init__(self, count, width, hidden):
        self.count, self.width, self.hidden = count, width, hidden
        self.place, self.size = {}, [0, 0, 0, 0]
        self.lanes = (width, 3 * width, hidden, width)
        self.put(0, OUTPUT_W, width)
        self.put(0, REDUCE_W, hidden)
        self.put(0, GRAD_MIXED, count)
        self.put(1, ATTEND_W, width)
        self.put(2, EXPAND_W, width)
        self.put(3, GRAD_RESID, count)
        self.put(3, MIXTURE, count)
        self.put(3, PARAMS, 16)
        for slot in range(2):
            for name in (FIRST, MIXED, SECOND, G_LOW, RESID_LOW):
                self.put(0, (name, slot), count)
            for name in (JOINED, GRAD_JOINED):
                self.put(1, (name, slot), count)
            for name in (SLOPE, PROBS, ACT, PRE_LOW):
                self.put(2, (name, slot), count)
            for name in (UNIT, UNIT_TWO, EDGE):
                self.put(3, (name, slot), count)
            self.put(3, (SUMS, slot), 16)
        self.room = {
            REDUCE: self.place[SLOPE, 0][:2],
            EXPAND: self.place[REDUCE_W][:2],
            ATTEND: (0, self.place[REDUCE_W][1] + hidden // 2),
            OUTPUT: self.place[OUTPUT_W][:2],
        }

    def put(self, arena, name, rows):
        self.place[name] = (arena, self.size[arena], rows)
        self.size[arena] += rows

    def shapes(self):
        return [pltpu.VMEM((rows, lanes), F32 if i == 3 else BF) for i, (rows, lanes) in enumerate(zip(self.size, self.lanes))]

    def views(self, arenas, slot=None):
        def view(name, slot=slot):
            arena, start, rows = self.place[name if name in self.place else (name, slot)]
            return arenas[arena].at[pl.ds(start, rows), :]

        return view

    def cut(self, arenas, name, slot):
        arena, start, rows = self.place[name, slot]
        return arenas[arena][start : start + rows]

    def lanes_of(self, name):
        return self.lanes[self.place[name, 0][0]]


def run(body, arenas, layout, ins=(), in_specs=(), outs=(), out_specs=(), scratch=(), name=None, weight=0, aliases=None):
    held = [] if arenas is None else [pinned(arena) for arena in arenas]
    given, kept = len(held) + len(ins), len(layout.lanes)

    def kernel(*refs):
        body(refs[given : given + kept], *refs[len(held) : given], *refs[given + kept :])

    result = pl.pallas_call(
        kernel,
        out_shape=layout.shapes() + list(outs),
        in_specs=[VM] * len(held) + list(in_specs),
        out_specs=[VM] * kept + list(out_specs),
        scratch_shapes=list(scratch),
        input_output_aliases={
            **{i: i for i in range(len(held))}, **{len(held) + i: kept + o for i, o in (aliases or {}).items()}
        },
        compiler_params=pltpu.CompilerParams(vmem_limit_bytes=LIMIT),
        cost_estimate=pl.CostEstimate(flops=1 + weight * 10**9, bytes_accessed=0, transcendentals=0),
        name=name,
    )(*held, *ins)
    return list(result[:kept]), list(result[kept:])


def group_bias(lengths_ref, micro, count):
    rows = lax.broadcasted_iota(jnp.int32, (count, count), 0)
    cols = lax.broadcasted_iota(jnp.int32, (count, count), 1)
    bound = jnp.int32(0)
    row_group = jnp.zeros((count, count), jnp.int32)
    col_group = jnp.zeros((count, count), jnp.int32)
    for crop in range(lengths_ref.shape[2]):
        bound = bound + lengths_ref[micro, 0, crop]
        row_group = row_group + (rows >= bound).astype(jnp.int32)
        col_group = col_group + (cols >= bound).astype(jnp.int32)
    return jnp.where(row_group == col_group, 0.0, -1e30).astype(F32)


def gelu_parts(pre):
    upper = 0.5 * (1.0 + lax.erf(pre * (2.0 ** -0.5)))
    return pre * upper, upper + pre * (jnp.exp(-0.5 * pre * pre) * 0.3989422804014327)


def norm_rows(values):
    center = values - jnp.mean(values, axis=-1, keepdims=True)
    factor = lax.rsqrt(jnp.mean(center * center, axis=-1, keepdims=True) + 1e-06)
    return center * factor, factor


def halves(count):
    lane = lax.broadcasted_iota(jnp.int32, (count, 128), 1)
    return lane < 64, lane >= 64


def factor_column(count, slot, norm):
    column = 2 * count + 128 * slot + norm
    return slice(column, column + 1)


def forward_body(view, slot, micro, a, low, ready):
    count, width = a.shape
    first, joined, probs, mixed, act, slope = (view(n) for n in (FIRST, JOINED, PROBS, MIXED, ACT, SLOPE))
    unit, unit_two, out, second, mixture, params = (view(n) for n in (UNIT, UNIT_TWO, EDGE, SECOND, MIXTURE, PARAMS))
    attend_w, output_w, expand_w, reduce_w = (view(n) for n in (ATTEND_W, OUTPUT_W, EXPAND_W, REDUCE_W))
    hidden = act.shape[1]
    bias = pl.ds(pl.multiple_of(micro * count, 128), count)

    def norm(source, unit, target, index):
        gain, shift = params[index : index + 1, :], params[2 + index : 3 + index, :]
        for r in range(0, count, ROWS):
            rows = pl.ds(r, ROWS)
            normed, factor = norm_rows(source[rows, :])
            unit[rows, :] = normed
            mixture[rows, factor_column(count, slot, index)] = factor
            target[rows, :] = (normed * gain + shift).astype(BF)

    ready(PARAMS, 0)
    norm(a, unit, first, 0)
    for i in range(3):
        ready(ATTEND_W, i)
        cols = pl.ds(i * width, width)
        part = dot(first[...], attend_w[:, cols])
        if i == 0:
            part = part + params[4:5, :]
        if i == 2:
            part = part + params[5:6, :]
        joined[:, cols] = part.astype(BF)

    ready(MIXTURE, 0)
    sides = halves(count)
    for pair in range(HEADS // 2):
        query = joined[:, pl.ds(pair * 128, 128)] * (64 ** -0.5)
        key = joined[:, pl.ds(width + pair * 128, 128)]
        value = joined[:, pl.ds(2 * width + pair * 128, 128)]
        total = None
        for half in range(2):
            scores = dot_nt(jnp.where(sides[half], query, 0).astype(BF), key) + mixture[:, bias]
            weights = jnp.exp(scores - jnp.max(scores, axis=-1, keepdims=True))
            prob = (weights * (1.0 / jnp.sum(weights, axis=-1, keepdims=True))).astype(BF)
            probs[:, pl.ds((2 * pair + half) * count, count)] = prob
            term = dot(prob, jnp.where(sides[half], value, 0).astype(BF))
            total = term if total is None else total + term
        mixed[:, pl.ds(pair * 128, 128)] = total.astype(BF)

    ready(OUTPUT_W, 0)
    out[...] = a[...] + dot(mixed[...], output_w[...]) + params[6:7, :]
    norm(out, unit_two, second, 1)
    for i in range(hidden // width):
        cols = pl.ds(i * width, width)
        ready(EXPAND_W, i)
        pre = dot(second[...], expand_w[:, cols]) + params[8 + i : 9 + i, :]
        value, grad = gelu_parts(pre)
        act[:, cols] = value.astype(BF)
        slope[:, cols] = grad.astype(BF)
        ready(REDUCE_W, i)
        out[...] += dot(act[:, cols], reduce_w[cols, :])
    out[...] += params[7:8, :]
    low[...] = out[...].astype(BF)


def forward_first(layout, ends, lengths, small, weights):
    count, width, hidden = layout.count, layout.width, layout.hidden
    tiles = hidden // width

    def body(arenas, ends, lengths, gains, shifts, offsets, bias, attend, output, expand, reduce, low, *scratch):
        a, lengths_s, gains_v, shifts_v, offsets_v, bias_v, sems, first_sems = scratch
        view = layout.views(arenas, 0)
        params, mixture = view(PARAMS), view(MIXTURE)
        attend_w, output_w, expand_w, reduce_w = (view(n) for n in (ATTEND_W, OUTPUT_W, EXPAND_W, REDUCE_W))
        early = [
            pltpu.make_async_copy(source, target, first_sems.at[i])
            for i, (source, target) in enumerate(
                [
                    (ends.at[0, 0], a), (gains, gains_v), (shifts, shifts_v), (lengths, lengths_s),
                    (offsets, offsets_v), (bias, bias_v),
                ]
            )
        ]
        copies = {}
        for i in range(3):
            cols = pl.ds(i * width, width)
            copies[ATTEND_W, i] = attend.at[0, :, cols], attend_w.at[:, cols]
        copies[OUTPUT_W, 0] = output.at[0], output_w
        for i in range(tiles):
            cols = pl.ds(i * width, width)
            copies[EXPAND_W, i] = expand.at[0, :, cols], expand_w.at[:, cols]
            copies[REDUCE_W, i] = reduce.at[0, cols], reduce_w.at[cols, :]
        for number, (name, pair) in enumerate(copies.items()):
            copies[name] = pltpu.make_async_copy(*pair, sems.at[number])
        order = list(copies)
        for copy in early:
            copy.start()
        for name in order[:4]:
            copies[name].start()

        def ready(name, i):
            if name == PARAMS:
                for copy in early:
                    copy.wait()
                params[0:2, :] = gains_v[0]
                params[2:4, :] = shifts_v[0]
                params[4:8, :] = offsets_v[0]
                for tile in range(tiles):
                    params[8 + tile : 9 + tile, :] = bias_v[0:1, pl.ds(tile * width, width)]
            elif name == MIXTURE:
                for micro in range(lengths.shape[0]):
                    mixture[:, pl.ds(micro * count, count)] = group_bias(lengths_s, micro, count)
            else:
                copies[name, i].wait()
                if (name, i) == (ATTEND_W, STAGE):
                    for later in order[4:]:
                        copies[later].start()

        section = lax.axis_index("section")
        pl.when(section == 0)(lambda: forward_body(view, 0, 0, a, low, ready))

        @pl.when(section != 0)
        def _():
            for name in ((PARAMS, 0), (MIXTURE, 0), *order):
                ready(*name)
            view(UNIT)[...] = a[...]

    return run(
        body, None, layout,
        ins=[in_hbm(v) for v in (ends, lengths, *small, *weights)], in_specs=[HB] * 10,
        outs=[pltpu.VMEM((count, width), BF)], out_specs=[VM],
        scratch=[
            pltpu.VMEM((count, width), F32), pltpu.SMEM(lengths.shape, jnp.int32),
            *[pltpu.VMEM(v.shape, F32) for v in small],
            pltpu.SemaphoreType.DMA((4 + 2 * tiles,)), pltpu.SemaphoreType.DMA((6,)),
        ],
        name="forward_first",
    )


def forward_later(layout, arenas, slot, own, ends, incoming):
    count, width = layout.count, layout.width

    def body(arenas, ends, incoming, low, a, sem):
        view = layout.views(arenas, slot)
        section = lax.axis_index("section")

        def step(micro):
            forward_body(view, slot, micro, a, low, lambda name, i: None)

        if own is None:
            @pl.when(section != 0)
            def _():
                copy = pltpu.make_async_copy(ends.at[0, ends.shape[1] - 1], view(UNIT, 1 - slot), sem)
                copy.start()
                a[...] = incoming[...].astype(F32)
                step(ends.shape[1] - 1)
                copy.wait()

            return

        @pl.when(section == 0)
        def _():
            copy = pltpu.make_async_copy(ends.at[0, own], a, sem)
            copy.start()
            copy.wait()

        @pl.when(section != 0)
        def _():
            a[...] = incoming[...].astype(F32)

        step(own - section)

    return run(
        body, arenas, layout, ins=[in_hbm(ends), pinned(incoming)], in_specs=[HB, VM],
        outs=[pltpu.VMEM((count, width), BF)], out_specs=[VM],
        scratch=[pltpu.VMEM((count, width), F32), pltpu.SemaphoreType.DMA], name="forward_later",
    )


def norm_back_all(grad, gain, normed_ref, factors, base, emit):
    count, width = normed_ref.shape
    sums = [jnp.zeros((8, width), F32)] * 3

    def fold(values):
        return jnp.sum(values.reshape(-1, 8, width), axis=0)

    for r in range(0, count, ROWS):
        rows = pl.ds(r, ROWS)
        part, normed = grad[rows, :], normed_ref[rows, :]
        scaled = part * gain
        result = base(rows) + factors(rows) * (
            scaled
            - jnp.mean(scaled, axis=-1, keepdims=True)
            - normed * jnp.mean(scaled * normed, axis=-1, keepdims=True)
        )
        sums = [total + fold(term) for total, term in zip(sums, (part * normed, part, result))]
        emit(rows, result)
    return [column_sum(total) for total in sums]


def column_sum(values):
    return jnp.sum(values, axis=0, keepdims=True)


def outer_body(view, slot, g, grad_second):
    count, width = g.shape
    slope, pre_low, g_low, resid_low, sums = (view(n) for n in (SLOPE, PRE_LOW, G_LOW, RESID_LOW, SUMS))
    grad_resid, mixture, params = view(GRAD_RESID), view(MIXTURE), view(PARAMS)
    output_w, expand_w, reduce_w = view(OUTPUT_W), view(EXPAND_W), view(REDUCE_W)
    hidden = slope.shape[1]
    g_low[...] = g[...].astype(BF)
    sums[7:8, :] = column_sum(g[...])
    for i in range(hidden // width):
        cols = pl.ds(i * width, width)
        grad_pre = dot_nt(g_low[...], reduce_w[cols, :]) * slope[:, cols].astype(F32)
        sums[8 + i : 9 + i, :] = column_sum(grad_pre)
        pre_low[:, cols] = grad_pre.astype(BF)
        term = dot_nt(pre_low[:, cols], expand_w[:, cols])
        if i == 0:
            grad_second[...] = term
        else:
            grad_second[...] += term

    def emit(rows, result):
        grad_resid[rows, :] = result
        resid_low[rows, :] = result.astype(BF)

    sums[1:2, :], sums[3:4, :], sums[6:7, :] = norm_back_all(
        grad_second, params[1:2, :], view(UNIT_TWO), lambda rows: mixture[rows, factor_column(count, slot, 1)],
        lambda rows: g[rows, :], emit,
    )
    view(GRAD_MIXED)[...] = dot_nt(resid_low[...], output_w[...]).astype(BF)


def inner_body(view, slot, low, grad_first):
    grad_resid, grad_mixed, joined, probs = view(GRAD_RESID), view(GRAD_MIXED), view(JOINED), view(PROBS)
    grad_joined, edge, sums = view(GRAD_JOINED), view(EDGE), view(SUMS)
    mixture, params, attend_w = view(MIXTURE), view(PARAMS), view(ATTEND_W)
    first_layer = lax.axis_index("section") == 0
    count, width = grad_resid.shape
    sides = halves(count)
    for pair in range(HEADS // 2):
        at = [pl.ds(j * width + pair * 128, 128) for j in range(3)]
        query, key, value = joined[:, at[0]] * (64 ** -0.5), joined[:, at[1]] * (64 ** -0.5), joined[:, at[2]]
        grad_out = grad_mixed[:, at[0]]
        totals = [None] * 3
        for half in range(2):
            side = sides[half]
            prob = probs[:, pl.ds((2 * pair + half) * count, count)]
            grad_half = jnp.where(side, grad_out, 0).astype(BF)
            grad_prob = dot_nt(grad_half, value)
            wide = prob.astype(F32)
            mass = wide * grad_prob
            grad_score = (mass - wide * jnp.sum(mass, axis=-1, keepdims=True)).astype(BF)
            terms = (
                dot(grad_score, jnp.where(side, key, 0).astype(BF)),
                dot_tn(grad_score, jnp.where(side, query, 0).astype(BF)),
                dot_tn(prob, grad_half),
            )
            totals = [t if old is None else old + t for old, t in zip(totals, terms)]
        for j in range(3):
            grad_joined[:, at[j]] = totals[j].astype(BF)
    sums[4:5, :] = column_sum(grad_joined[:, pl.ds(0, width)].astype(F32))
    sums[5:6, :] = column_sum(grad_joined[:, pl.ds(2 * width, width)].astype(F32))
    grad_first[...] = dot_nt(grad_joined[...], attend_w[...])

    def emit(rows, result):
        edge[rows, :] = jnp.where(first_layer, result, edge[rows, :])
        low[rows, :] = result.astype(BF)

    sums[0:1, :], sums[2:3, :], _ = norm_back_all(
        grad_first, params[0:1, :], view(UNIT), lambda rows: mixture[rows, factor_column(count, slot, 0)],
        lambda rows: grad_resid[rows, :], emit,
    )


def only_on(only, step):
    if only is None:
        step()
    else:
        pl.when(lax.axis_index("section") == only)(step)


def backward_outer(layout, arenas, slot, only, incoming):
    count, width = layout.count, layout.width

    def body(arenas, incoming, g, grad_second):
        view = layout.views(arenas, slot)
        section = lax.axis_index("section")

        def step():
            if only != 0:
                @pl.when(section != 0)
                def _():
                    g[...] = view(UNIT, 1 - slot)[...]
            if only != 1:
                @pl.when(section == 0)
                def _():
                    g[...] = incoming[...].astype(F32)
            outer_body(view, slot, g, grad_second)

        only_on(only, step)

    return run(
        body, arenas, layout, ins=[pinned(incoming)], in_specs=[VM],
        scratch=[pltpu.VMEM((count, width), F32), pltpu.VMEM((count, width), F32)], name="backward_outer",
    )[0]


def backward_inner(layout, arenas, slot, only):
    count, width = layout.count, layout.width

    def body(arenas, low, grad_first):
        only_on(only, lambda: inner_body(layout.views(arenas, slot), slot, low, grad_first))

    return run(
        body, arenas, layout, outs=[pltpu.VMEM((count, width), BF)], out_specs=[VM],
        scratch=[pltpu.VMEM((count, width), F32)], name="backward_inner",
    )


def edges_of(layout, arenas):
    def body(arenas, edges, sems):
        view = layout.views(arenas)

        def move(slots):
            copies = [pltpu.make_async_copy(view(EDGE, slot), edges.at[0, i], sems.at[i]) for i, slot in enumerate(slots)]
            for copy in copies:
                copy.start()
            for copy in copies:
                copy.wait()

        section = lax.axis_index("section")
        pl.when(section == 0)(lambda: move((0, 1)))
        pl.when(section != 0)(lambda: move((1, 0)))

    arenas, (edges,) = run(
        body, arenas, layout, outs=[jax.ShapeDtypeStruct((1, 2, layout.count, layout.width), F32)], out_specs=[HB],
        scratch=[pltpu.SemaphoreType.DMA((2,))], name="edges",
    )
    return arenas, edges


FACTORS = {
    REDUCE: (G_LOW, ACT, 8), EXPAND: (PRE_LOW, SECOND, 2), ATTEND: (GRAD_JOINED, FIRST, 4), OUTPUT: (RESID_LOW, MIXED, 8)
}


def spread(sums, place, devices, hidden, lanes):
    width = sums.shape[1]
    share, wide = width // devices, hidden // devices
    bias = 8 + place * wide // width
    rows = (sums[:8], jnp.broadcast_to(sums[bias : bias + 1], (8, width)))
    starts = (place * share, place * wide % width)
    return jnp.concatenate([pltpu.roll(row, (width - start) % width, 1) for row, start in zip(rows, starts)])[:, :lanes]


class Share:
    def __init__(self, layout, devices, name, part, parts, order):
        left, right, self.per = FACTORS[name]
        self.layout, self.name, self.left, self.right = layout, name, left, right
        self.extra = name == ATTEND and part == 0
        self.own = layout.lanes_of(left) // devices
        self.rows = self.own + (16 if self.extra else 0)
        self.full = layout.lanes_of(right)
        self.columns = self.full // parts
        self.lanes = pl.ds(part * self.columns, self.columns)
        self.pairs = devices // 2
        self.todo, self.free = list(order), list(range(self.pairs.bit_length() - 1))
        self.total = None

    def block(self, arenas, pair):
        arena, start = self.layout.room[self.name]
        row = start + pair * (self.own + (16 if self.name == ATTEND else 0))
        return arenas[arena].at[pl.ds(row if isinstance(row, int) else pl.multiple_of(row, 16), self.rows), self.lanes]

    def make(self, arenas, incoming=None):
        ins = [] if incoming is None else [pinned(incoming)]

        def body(arenas, *refs):
            *given, send = refs
            core = lax.rem(lax.axis_index("dp"), 2)
            if given:
                @pl.when(lax.axis_index("section") == 0)
                def _():
                    self.layout.views(arenas)(G_LOW, 1)[...] = given[0][...]

            if self.extra:
                view = self.layout.views(arenas)
                sums = view(SUMS, 0)[...] + view(SUMS, 1)[...]
                for pair in range(self.pairs):
                    low, high = (
                        spread(sums, 2 * pair + half, 2 * self.pairs, self.layout.hidden, self.columns) for half in range(2)
                    )
                    for target, half in ((self.block(arenas, pair), core), (send.at[pair], 1 - core)):
                        target[self.own :, :] = jnp.where(half == 0, low, high).astype(BF)

            per = min(self.per, self.pairs)
            for start in range(0, self.pairs, per):
                rows = pl.ds(2 * start * self.own, 2 * per * self.own)
                total = None
                for slot in range(2):
                    view = self.layout.views(arenas, slot)
                    term = dot_tn(view(self.left)[:, rows], view(self.right)[:, self.lanes])
                    total = term if total is None else total + term
                total = total.astype(BF).reshape(per, 2, self.own, self.columns)
                for j in range(per):
                    self.block(arenas, start + j)[: self.own, :] = jnp.where(core == 0, total[j, 0], total[j, 1])
                    send[start + j, : self.own, :] = jnp.where(core == 0, total[j, 1], total[j, 0])

        arenas, (send,) = run(
            body, arenas, self.layout, ins=ins, in_specs=[VM] * len(ins),
            outs=[pltpu.VMEM((self.pairs, self.rows, self.columns), BF)], out_specs=[VM], name="product",
        )
        self.moved = exchanged(send, 1)
        return arenas

    def step(self, arenas, totals):
        free, done = list(self.free), [place for place in range(self.pairs.bit_length() - 1) if place not in self.free]
        bit = self.todo.pop(0) if self.todo else None
        place = None if bit is None else bit.bit_length() - 2
        rest = [p for p in free if p != place]
        earlier = totals.get(self.name) if place is None else None

        def body(arenas, moved, *refs):
            device = lax.axis_index("dp")

            def mine(place):
                return lax.rem(lax.div(device, 2 << place), 2)

            base = sum((mine(p) << p for p in done), 0)

            def spot(number, side):
                bits = {p: (number >> k) & 1 for k, p in enumerate(rest)}
                if place is not None:
                    bits[place] = side
                index = sum((bits[p] << k for k, p in enumerate(free)), 0)
                return base + sum((bits[p] << p for p in free), 0), index

            if place is None:
                pair, index = spot(0, None)
                total = self.block(arenas, pair)[...].astype(F32) + moved[index].astype(F32)
                self.finish(total, *refs[0 if earlier is None else 1 :])
                return
            target, side = refs[0], mine(place)
            for number in range(1 << len(rest)):
                pair, index = spot(number, 1 - side)
                target[number] = self.block(arenas, pair)[...] + moved[index]
                pair, index = spot(number, side)
                block = self.block(arenas, pair)
                block[...] = block[...] + moved[index]

        ins = [] if earlier is None else [in_hbm(earlier)]
        if place is None:
            share = self.layout.width // (2 * self.pairs)
            outs, out_specs = [jax.ShapeDtypeStruct((self.own, self.full), F32)], [HB]
            scratch = [pltpu.VMEM((self.own, self.columns), F32), pltpu.SemaphoreType.DMA]
            if self.extra:
                outs += [jax.ShapeDtypeStruct((1, n, share), F32) for n in (2, 2, 4)]
                outs += [jax.ShapeDtypeStruct((1, self.layout.hidden // (2 * self.pairs)), F32)]
                out_specs += [VM] * 4
        else:
            outs, out_specs, scratch = [pltpu.VMEM((1 << len(rest), self.rows, self.columns), BF)], [VM], []
        arenas, results = run(
            body, arenas, self.layout, ins=[pinned(self.moved), *ins], in_specs=[VM] + [HB] * len(ins), outs=outs,
            out_specs=out_specs, scratch=scratch, name="add", weight=30, aliases={1: 0} if ins else {},
        )
        if place is None:
            totals[self.name] = results[0]
            if self.extra:
                totals[None] = results[1:]
        else:
            self.moved = exchanged(results[0], bit)
            self.free = rest
        return arenas

    def finish(self, total, *refs):
        *refs, held, sem = refs
        held[...] = total[: self.own]
        copy = pltpu.make_async_copy(held, refs[0].at[:, self.lanes], sem)
        copy.start()
        if self.extra:
            small, start = total[self.own :], 0
            for target in refs[1:4]:
                count, share = target.shape[1:]
                target[0] = small[start : start + count, :share]
                start += count
            refs[4][...] = small[8:9, : refs[4].shape[1]]
        copy.wait()


def shifted(value, axis, by):
    devices = lax.axis_size(axis)
    pairs = [(i, i + by) for i in range(devices) if 0 <= i + by < devices]
    return lax.ppermute(value, axis, pairs)


def exchanged(value, bit):
    return lax.ppermute(value, "dp", [(i, i ^ bit) for i in range(lax.axis_size("dp"))])


UP, SIDE = (2, 4, 8), (4, 8, 2)
PARTS = (
    (REDUCE, 0, 2, UP), (REDUCE, 1, 2, UP), (EXPAND, 0, 2, UP), (EXPAND, 1, 2, SIDE), (ATTEND, 0, 2, UP), (ATTEND, 1, 2, UP), (OUTPUT, 0, 1, UP)
)
OUTER, INNER, EDGES = -1, -2, -3
TURNS = (0, OUTER, 3, 0, 1, 3, 2, 1, INNER, 0, 5, 3, 5, 2, 1, 0, EDGES, 5, 3, 1, 0, 4, 5, 4, 2, 3, 6, 1, 5, 6, 2, 4, 6, 2, 4, 6, 4, 6)


def shards(
    ends, lengths, norm_gains, norm_shifts, attend_weight, offsets, output_weight, expand_weight, expand_bias, reduce_weight
):
    devices = lax.axis_size("dp")
    count, width = ends.shape[2:]
    hidden = expand_weight.shape[2]
    layout = Layout(count, width, hidden)
    small = (norm_gains, norm_shifts, offsets, expand_bias)
    weights = (attend_weight, output_weight, expand_weight, reduce_weight)

    arenas, (low,) = forward_first(layout, ends, lengths, small, weights)
    incoming = shifted(low, "section", 1)
    arenas, (low,) = forward_later(layout, arenas, 1, 1, ends, incoming)
    later = shifted(low, "section", 1)
    arenas = backward_outer(layout, arenas, 1, 1, incoming)
    arenas, (low,) = backward_inner(layout, arenas, 1, 1)
    grad_zero = shifted(low, "section", -1)
    arenas, _ = forward_later(layout, arenas, 0, None, ends, later)
    arenas = backward_outer(layout, arenas, 0, None, grad_zero)
    arenas, (low,) = backward_inner(layout, arenas, 0, None)
    grad_one = shifted(low, "section", -1)

    if devices == 16:
        shares = [Share(layout, devices, *part) for part in PARTS]
        made, totals = set(), {}
        for turn in TURNS:
            if turn == OUTER:
                arenas = backward_outer(layout, arenas, 1, 0, grad_one)
            elif turn == INNER:
                arenas, _ = backward_inner(layout, arenas, 1, 0)
            elif turn == EDGES:
                arenas, edges = edges_of(layout, arenas)
            elif turn in made:
                arenas = shares[turn].step(arenas, totals)
            else:
                arenas = shares[turn].make(arenas, None if made else grad_one)
                made.add(turn)
        gains, shifts, offset_grads, bias = totals[None]
        grads = {name: totals[name].T[None] for name in FACTORS}
    else:
        arenas = backward_outer(layout, arenas, 1, 0, grad_one)
        arenas, _ = backward_inner(layout, arenas, 1, 0)
        arenas, edges = edges_of(layout, arenas)
        sums = layout.cut(arenas, SUMS, 0) + layout.cut(arenas, SUMS, 1)
        grads = {}
        for name, (left, right, _) in FACTORS.items():
            term = sum(dot_tn(layout.cut(arenas, right, s), layout.cut(arenas, left, s)) for s in range(2)).astype(BF)
            grads[name] = lax.psum_scatter(term, "dp", scatter_dimension=1, tiled=True).astype(F32)[None]
        bias = sums[8 : 8 + hidden // width].reshape(width, hidden // width)
        little = lax.psum_scatter(jnp.concatenate([sums[:8].T, bias], axis=1), "dp", scatter_dimension=0, tiled=True)
        gains, shifts, offset_grads = (little[:, i:j].T[None] for i, j in ((0, 2), (2, 4), (4, 8)))
        bias = little[:, 8:].reshape(1, -1)
    return edges, gains, shifts, grads[ATTEND], offset_grads, grads[OUTPUT], grads[EXPAND], bias, grads[REDUCE]


def solution(mesh):
    in_specs = (
        P("section", None, "dp", None),
        P(None, "dp", None),
        P("section", None, None),
        P("section", None, None),
        P("section", None, None),
        P("section", None, None),
        P("section", None, None),
        P("section", None, None),
        P("section", None),
        P("section", None, None),
    )
    out_specs = (
        P("section", None, "dp", None),
        P("section", None, "dp"),
        P("section", None, "dp"),
        P("section", None, "dp"),
        P("section", None, "dp"),
        P("section", None, "dp"),
        P("section", None, "dp"),
        P("section", "dp"),
        P("section", None, "dp"),
    )
    return jax.shard_map(shards, mesh=mesh, in_specs=in_specs, out_specs=out_specs, check_vma=False)
```

```python
import jax
import jax.numpy as jnp
from jax import lax
from jax.experimental import pallas as pl
from jax.experimental.pallas import tpu as pltpu
from jax.sharding import PartitionSpec as P

HEADS = 12
STAGE = 0
ROWS = 32
LIMIT = 7 * 2**20
BF = jnp.bfloat16
F32 = jnp.float32
VM = pl.BlockSpec(memory_space=pltpu.VMEM)
HB = pl.BlockSpec(memory_space=pltpu.HBM)

SLOTTED = (
    FIRST, MIXED, SECOND, G_LOW, RESID_LOW, JOINED, GRAD_JOINED, SLOPE, PROBS, ACT, PRE_LOW, UNIT, UNIT_TWO, EDGE, SUMS
) = range(15)
SHARED = OUTPUT_W, REDUCE_W, GRAD_MIXED, ATTEND_W, EXPAND_W, GRAD_RESID, MIXTURE, PARAMS = range(15, 23)
REDUCE, EXPAND, ATTEND, OUTPUT = range(4)


def in_hbm(value):
    return pltpu.with_memory_space_constraint(value, pltpu.HBM)


def pinned(value):
    return pltpu.with_memory_space_constraint(value, pltpu.VMEM)


def dot(left, right, dims=((1,), (0,))):
    return lax.dot_general(left, right, (dims, ((), ())), preferred_element_type=F32)


def dot_nt(left, right):
    return dot(left, right, ((1,), (1,)))


def dot_tn(left, right):
    return dot(left, right, ((0,), (0,)))


class Layout:
    def __init__(self, count, width, hidden):
        self.count, self.width, self.hidden = count, width, hidden
        self.place, self.size = {}, [0, 0, 0, 0]
        self.lanes = (width, 3 * width, hidden, width)
        self.put(0, OUTPUT_W, width)
        self.put(0, REDUCE_W, hidden)
        self.put(0, GRAD_MIXED, count)
        self.put(1, ATTEND_W, width)
        self.put(2, EXPAND_W, width)
        self.put(3, GRAD_RESID, count)
        self.put(3, MIXTURE, count)
        self.put(3, PARAMS, 16)
        for slot in range(2):
            for name in (FIRST, MIXED, SECOND, G_LOW, RESID_LOW):
                self.put(0, (name, slot), count)
            for name in (JOINED, GRAD_JOINED):
                self.put(1, (name, slot), count)
            for name in (SLOPE, PROBS, ACT, PRE_LOW):
                self.put(2, (name, slot), count)
            for name in (UNIT, UNIT_TWO, EDGE):
                self.put(3, (name, slot), count)
            self.put(3, (SUMS, slot), 16)
        self.room = {
            REDUCE: self.place[SLOPE, 0][:2],
            EXPAND: self.place[REDUCE_W][:2],
            ATTEND: (0, self.place[REDUCE_W][1] + hidden // 2),
            OUTPUT: self.place[OUTPUT_W][:2],
        }

    def put(self, arena, name, rows):
        self.place[name] = (arena, self.size[arena], rows)
        self.size[arena] += rows

    def shapes(self):
        return [pltpu.VMEM((rows, lanes), F32 if i == 3 else BF) for i, (rows, lanes) in enumerate(zip(self.size, self.lanes))]

    def views(self, arenas, slot=None):
        def view(name, slot=slot):
            arena, start, rows = self.place[name if name in self.place else (name, slot)]
            return arenas[arena].at[pl.ds(start, rows), :]

        return view

    def cut(self, arenas, name, slot):
        arena, start, rows = self.place[name, slot]
        return arenas[arena][start : start + rows]

    def lanes_of(self, name):
        return self.lanes[self.place[name, 0][0]]


def run(body, arenas, layout, ins=(), in_specs=(), outs=(), out_specs=(), scratch=(), name=None, weight=0, aliases=None):
    held = [] if arenas is None else [pinned(arena) for arena in arenas]
    given, kept = len(held) + len(ins), len(layout.lanes)

    def kernel(*refs):
        body(refs[given : given + kept], *refs[len(held) : given], *refs[given + kept :])

    result = pl.pallas_call(
        kernel,
        out_shape=layout.shapes() + list(outs),
        in_specs=[VM] * len(held) + list(in_specs),
        out_specs=[VM] * kept + list(out_specs),
        scratch_shapes=list(scratch),
        input_output_aliases={
            **{i: i for i in range(len(held))}, **{len(held) + i: kept + o for i, o in (aliases or {}).items()}
        },
        compiler_params=pltpu.CompilerParams(vmem_limit_bytes=LIMIT),
        cost_estimate=pl.CostEstimate(flops=1 + weight * 10**9, bytes_accessed=0, transcendentals=0),
        name=name,
    )(*held, *ins)
    return list(result[:kept]), list(result[kept:])


def group_bias(lengths_ref, micro, count):
    rows = lax.broadcasted_iota(jnp.int32, (count, count), 0)
    cols = lax.broadcasted_iota(jnp.int32, (count, count), 1)
    bound = jnp.int32(0)
    row_group = jnp.zeros((count, count), jnp.int32)
    col_group = jnp.zeros((count, count), jnp.int32)
    for crop in range(lengths_ref.shape[2]):
        bound = bound + lengths_ref[micro, 0, crop]
        row_group = row_group + (rows >= bound).astype(jnp.int32)
        col_group = col_group + (cols >= bound).astype(jnp.int32)
    return jnp.where(row_group == col_group, 0.0, -1e30).astype(F32)


def gelu_parts(pre):
    upper = 0.5 * (1.0 + lax.erf(pre * (2.0 ** -0.5)))
    return pre * upper, upper + pre * (jnp.exp(-0.5 * pre * pre) * 0.3989422804014327)


def norm_rows(values):
    center = values - jnp.mean(values, axis=-1, keepdims=True)
    factor = lax.rsqrt(jnp.mean(center * center, axis=-1, keepdims=True) + 1e-06)
    return center * factor, factor


def halves(count):
    lane = lax.broadcasted_iota(jnp.int32, (count, 128), 1)
    return lane < 64, lane >= 64


def factor_column(count, slot, norm):
    column = 2 * count + 128 * slot + norm
    return slice(column, column + 1)


def forward_body(view, slot, micro, a, low, ready):
    count, width = a.shape
    first, joined, probs, mixed, act, slope = (view(n) for n in (FIRST, JOINED, PROBS, MIXED, ACT, SLOPE))
    unit, unit_two, out, second, mixture, params = (view(n) for n in (UNIT, UNIT_TWO, EDGE, SECOND, MIXTURE, PARAMS))
    attend_w, output_w, expand_w, reduce_w = (view(n) for n in (ATTEND_W, OUTPUT_W, EXPAND_W, REDUCE_W))
    hidden = act.shape[1]
    bias = pl.ds(micro * count, count)

    def norm(source, unit, target, index):
        gain, shift = params[index : index + 1, :], params[2 + index : 3 + index, :]
        for r in range(0, count, ROWS):
            rows = pl.ds(r, ROWS)
            normed, factor = norm_rows(source[rows, :])
            unit[rows, :] = normed
            mixture[rows, factor_column(count, slot, index)] = factor
            target[rows, :] = (normed * gain + shift).astype(BF)

    ready(PARAMS, 0)
    norm(a, unit, first, 0)
    for i in range(3):
        ready(ATTEND_W, i)
        cols = pl.ds(i * width, width)
        part = dot(first[...], attend_w[:, cols])
        if i == 0:
            part = part + params[4:5, :]
        if i == 2:
            part = part + params[5:6, :]
        joined[:, cols] = part.astype(BF)

    ready(MIXTURE, 0)
    sides = halves(count)
    for pair in range(HEADS // 2):
        query = joined[:, pl.ds(pair * 128, 128)] * (64 ** -0.5)
        key = joined[:, pl.ds(width + pair * 128, 128)]
        value = joined[:, pl.ds(2 * width + pair * 128, 128)]
        total = None
        for half in range(2):
            scores = dot_nt(jnp.where(sides[half], query, 0).astype(BF), key) + mixture[:, bias]
            weights = jnp.exp(scores - jnp.max(scores, axis=-1, keepdims=True))
            prob = (weights * (1.0 / jnp.sum(weights, axis=-1, keepdims=True))).astype(BF)
            probs[:, pl.ds((2 * pair + half) * count, count)] = prob
            term = dot(prob, jnp.where(sides[half], value, 0).astype(BF))
            total = term if total is None else total + term
        mixed[:, pl.ds(pair * 128, 128)] = total.astype(BF)

    ready(OUTPUT_W, 0)
    out[...] = a[...] + dot(mixed[...], output_w[...]) + params[6:7, :]
    norm(out, unit_two, second, 1)
    for i in range(hidden // width):
        cols = pl.ds(i * width, width)
        ready(EXPAND_W, i)
        pre = dot(second[...], expand_w[:, cols]) + params[8 + i : 9 + i, :]
        value, grad = gelu_parts(pre)
        act[:, cols] = value.astype(BF)
        slope[:, cols] = grad.astype(BF)
        ready(REDUCE_W, i)
        out[...] += dot(act[:, cols], reduce_w[cols, :])
    out[...] += params[7:8, :]
    low[...] = out[...].astype(BF)


def forward_first(layout, ends, lengths, small, weights):
    count, width, hidden = layout.count, layout.width, layout.hidden
    tiles = hidden // width

    def body(arenas, ends, lengths, gains, shifts, offsets, bias, attend, output, expand, reduce, low, *scratch):
        a, lengths_s, gains_v, shifts_v, offsets_v, bias_v, sems, first_sems = scratch
        view = layout.views(arenas, 0)
        params, mixture = view(PARAMS), view(MIXTURE)
        attend_w, output_w, expand_w, reduce_w = (view(n) for n in (ATTEND_W, OUTPUT_W, EXPAND_W, REDUCE_W))
        early = [
            pltpu.make_async_copy(source, target, first_sems.at[i])
            for i, (source, target) in enumerate(
                [
                    (ends.at[0, 0], a), (gains, gains_v), (shifts, shifts_v), (lengths, lengths_s),
                    (offsets, offsets_v), (bias, bias_v),
                ]
            )
        ]
        copies = {}
        for i in range(3):
            cols = pl.ds(i * width, width)
            copies[ATTEND_W, i] = attend.at[0, :, cols], attend_w.at[:, cols]
        copies[OUTPUT_W, 0] = output.at[0], output_w
        for i in range(tiles):
            cols = pl.ds(i * width, width)
            copies[EXPAND_W, i] = expand.at[0, :, cols], expand_w.at[:, cols]
            copies[REDUCE_W, i] = reduce.at[0, cols], reduce_w.at[cols, :]
        for number, (name, pair) in enumerate(copies.items()):
            copies[name] = pltpu.make_async_copy(*pair, sems.at[number])
        order = list(copies)
        for copy in early:
            copy.start()
        for name in order[:4]:
            copies[name].start()

        def ready(name, i):
            if name == PARAMS:
                for copy in early:
                    copy.wait()
                params[0:2, :] = gains_v[0]
                params[2:4, :] = shifts_v[0]
                params[4:8, :] = offsets_v[0]
                for tile in range(tiles):
                    params[8 + tile : 9 + tile, :] = bias_v[0:1, pl.ds(tile * width, width)]
            elif name == MIXTURE:
                for micro in range(lengths.shape[0]):
                    mixture[:, pl.ds(micro * count, count)] = group_bias(lengths_s, micro, count)
            else:
                copies[name, i].wait()
                if (name, i) == (ATTEND_W, STAGE):
                    for later in order[4:]:
                        copies[later].start()

        section = lax.axis_index("section")
        pl.when(section == 0)(lambda: forward_body(view, 0, 0, a, low, ready))

        @pl.when(section != 0)
        def _():
            for name in ((PARAMS, 0), (MIXTURE, 0), *order):
                ready(*name)
            view(UNIT)[...] = a[...]

    return run(
        body, None, layout,
        ins=[in_hbm(v) for v in (ends, lengths, *small, *weights)], in_specs=[HB] * 10,
        outs=[pltpu.VMEM((count, width), BF)], out_specs=[VM],
        scratch=[
            pltpu.VMEM((count, width), F32), pltpu.SMEM(lengths.shape, jnp.int32),
            *[pltpu.VMEM(v.shape, F32) for v in small],
            pltpu.SemaphoreType.DMA((4 + 2 * tiles,)), pltpu.SemaphoreType.DMA((6,)),
        ],
        name="forward_first",
    )


def forward_later(layout, arenas, slot, side, micro, ends, incoming=None, take=False):
    count, width = layout.count, layout.width
    ins = [in_hbm(ends)] + ([] if incoming is None else [pinned(incoming)])

    def body(arenas, ends, *refs):
        *given, low, a, sem = refs
        view = layout.views(arenas, slot)

        def step():
            forward_body(view, slot, micro, a, low, lambda name, i: None)

        @pl.when(lax.axis_index("section") == side)
        def _():
            if not given:
                copy = pltpu.make_async_copy(ends.at[0, micro], a, sem)
                copy.start()
                copy.wait()
                step()
                return
            if take:
                copy = pltpu.make_async_copy(ends.at[0, ends.shape[1] - 1], view(UNIT, 1 - slot), sem)
                copy.start()
            a[...] = given[0][...].astype(F32)
            step()
            if take:
                copy.wait()

    return run(
        body, arenas, layout, ins=ins, in_specs=[HB, VM][: len(ins)],
        outs=[pltpu.VMEM((count, width), BF)], out_specs=[VM],
        scratch=[pltpu.VMEM((count, width), F32), pltpu.SemaphoreType.DMA], name="forward_later",
    )


def norm_back_all(grad, gain, normed_ref, factors, base, emit):
    count, width = normed_ref.shape
    sums = [jnp.zeros((8, width), F32)] * 3

    def fold(values):
        return jnp.sum(values.reshape(-1, 8, width), axis=0)

    for r in range(0, count, ROWS):
        rows = pl.ds(r, ROWS)
        part, normed = grad[rows, :], normed_ref[rows, :]
        scaled = part * gain
        result = base(rows) + factors(rows) * (
            scaled
            - jnp.mean(scaled, axis=-1, keepdims=True)
            - normed * jnp.mean(scaled * normed, axis=-1, keepdims=True)
        )
        sums = [total + fold(term) for total, term in zip(sums, (part * normed, part, result))]
        emit(rows, result)
    return [column_sum(total) for total in sums]


def column_sum(values):
    return jnp.sum(values, axis=0, keepdims=True)


def outer_body(view, slot, g, grad_second):
    count, width = g.shape
    slope, pre_low, g_low, resid_low, sums = (view(n) for n in (SLOPE, PRE_LOW, G_LOW, RESID_LOW, SUMS))
    grad_resid, mixture, params = view(GRAD_RESID), view(MIXTURE), view(PARAMS)
    output_w, expand_w, reduce_w = view(OUTPUT_W), view(EXPAND_W), view(REDUCE_W)
    hidden = slope.shape[1]
    g_low[...] = g[...].astype(BF)
    sums[7:8, :] = column_sum(g[...])
    for i in range(hidden // width):
        cols = pl.ds(i * width, width)
        grad_pre = dot_nt(g_low[...], reduce_w[cols, :]) * slope[:, cols].astype(F32)
        sums[8 + i : 9 + i, :] = column_sum(grad_pre)
        pre_low[:, cols] = grad_pre.astype(BF)
        term = dot_nt(pre_low[:, cols], expand_w[:, cols])
        if i == 0:
            grad_second[...] = term
        else:
            grad_second[...] += term

    def emit(rows, result):
        grad_resid[rows, :] = result
        resid_low[rows, :] = result.astype(BF)

    sums[1:2, :], sums[3:4, :], sums[6:7, :] = norm_back_all(
        grad_second, params[1:2, :], view(UNIT_TWO), lambda rows: mixture[rows, factor_column(count, slot, 1)],
        lambda rows: g[rows, :], emit,
    )
    view(GRAD_MIXED)[...] = dot_nt(resid_low[...], output_w[...]).astype(BF)


def inner_body(view, slot, low, grad_first):
    grad_resid, grad_mixed, joined, probs = view(GRAD_RESID), view(GRAD_MIXED), view(JOINED), view(PROBS)
    grad_joined, edge, sums = view(GRAD_JOINED), view(EDGE), view(SUMS)
    mixture, params, attend_w = view(MIXTURE), view(PARAMS), view(ATTEND_W)
    first_layer = lax.axis_index("section") == 0
    count, width = grad_resid.shape
    sides = halves(count)
    for pair in range(HEADS // 2):
        at = [pl.ds(j * width + pair * 128, 128) for j in range(3)]
        query, key, value = joined[:, at[0]] * (64 ** -0.5), joined[:, at[1]] * (64 ** -0.5), joined[:, at[2]]
        grad_out = grad_mixed[:, at[0]]
        totals = [None] * 3
        for half in range(2):
            side = sides[half]
            prob = probs[:, pl.ds((2 * pair + half) * count, count)]
            grad_half = jnp.where(side, grad_out, 0).astype(BF)
            grad_prob = dot_nt(grad_half, value)
            wide = prob.astype(F32)
            mass = wide * grad_prob
            grad_score = (mass - wide * jnp.sum(mass, axis=-1, keepdims=True)).astype(BF)
            terms = (
                dot(grad_score, jnp.where(side, key, 0).astype(BF)),
                dot_tn(grad_score, jnp.where(side, query, 0).astype(BF)),
                dot_tn(prob, grad_half),
            )
            totals = [t if old is None else old + t for old, t in zip(totals, terms)]
        for j in range(3):
            grad_joined[:, at[j]] = totals[j].astype(BF)
    sums[4:5, :] = column_sum(grad_joined[:, pl.ds(0, width)].astype(F32))
    sums[5:6, :] = column_sum(grad_joined[:, pl.ds(2 * width, width)].astype(F32))
    grad_first[...] = dot_nt(grad_joined[...], attend_w[...])

    def emit(rows, result):
        edge[rows, :] = jnp.where(first_layer, result, edge[rows, :])
        low[rows, :] = result.astype(BF)

    sums[0:1, :], sums[2:3, :], _ = norm_back_all(
        grad_first, params[0:1, :], view(UNIT), lambda rows: mixture[rows, factor_column(count, slot, 0)],
        lambda rows: grad_resid[rows, :], emit,
    )


def backward_outer(layout, arenas, slot, side, incoming=None):
    count, width = layout.count, layout.width
    ins = [] if incoming is None else [pinned(incoming)]

    def body(arenas, *refs):
        *given, g, grad_second = refs
        view = layout.views(arenas, slot)

        @pl.when(lax.axis_index("section") == side)
        def _():
            g[...] = given[0][...].astype(F32) if given else view(UNIT, 1 - slot)[...]
            outer_body(view, slot, g, grad_second)

    return run(
        body, arenas, layout, ins=ins, in_specs=[VM] * len(ins),
        scratch=[pltpu.VMEM((count, width), F32), pltpu.VMEM((count, width), F32)], name="backward_outer",
    )[0]


def backward_inner(layout, arenas, slot, side):
    count, width = layout.count, layout.width

    def body(arenas, low, grad_first):
        @pl.when(lax.axis_index("section") == side)
        def _():
            inner_body(layout.views(arenas, slot), slot, low, grad_first)

    return run(
        body, arenas, layout, outs=[pltpu.VMEM((count, width), BF)], out_specs=[VM],
        scratch=[pltpu.VMEM((count, width), F32)], name="backward_inner",
    )


def edges_of(layout, arenas):
    def body(arenas, edges, sems):
        view = layout.views(arenas)

        def move(slots):
            copies = [pltpu.make_async_copy(view(EDGE, slot), edges.at[0, i], sems.at[i]) for i, slot in enumerate(slots)]
            for copy in copies:
                copy.start()
            for copy in copies:
                copy.wait()

        section = lax.axis_index("section")
        pl.when(section == 0)(lambda: move((0, 1)))
        pl.when(section != 0)(lambda: move((1, 0)))

    arenas, (edges,) = run(
        body, arenas, layout, outs=[jax.ShapeDtypeStruct((1, 2, layout.count, layout.width), F32)], out_specs=[HB],
        scratch=[pltpu.SemaphoreType.DMA((2,))], name="edges",
    )
    return arenas, edges


FACTORS = {
    REDUCE: (G_LOW, ACT, 8), EXPAND: (PRE_LOW, SECOND, 2), ATTEND: (GRAD_JOINED, FIRST, 4), OUTPUT: (RESID_LOW, MIXED, 8)
}


def spread(sums, place, devices, hidden, lanes):
    width = sums.shape[1]
    share, wide = width // devices, hidden // devices
    bias = 8 + place * wide // width
    rows = (sums[:8], jnp.broadcast_to(sums[bias : bias + 1], (8, width)))
    starts = (place * share, place * wide % width)
    return jnp.concatenate([pltpu.roll(row, (width - start) % width, 1) for row, start in zip(rows, starts)])[:, :lanes]


class Share:
    def __init__(self, layout, devices, name, part, parts, order):
        left, right, self.per = FACTORS[name]
        self.layout, self.name, self.left, self.right = layout, name, left, right
        self.extra = name == ATTEND and part == 0
        self.own = layout.lanes_of(left) // devices
        self.rows = self.own + (16 if self.extra else 0)
        self.full = layout.lanes_of(right)
        self.columns = self.full // parts
        self.lanes = pl.ds(part * self.columns, self.columns)
        self.pairs = devices // 2
        self.todo, self.free = list(order), list(range(self.pairs.bit_length() - 1))
        self.total = None

    def block(self, arenas, pair):
        arena, start = self.layout.room[self.name]
        row = start + pair * (self.own + (16 if self.name == ATTEND else 0))
        return arenas[arena].at[pl.ds(row if isinstance(row, int) else pl.multiple_of(row, 16), self.rows), self.lanes]

    def make(self, arenas, incoming=None):
        ins = [] if incoming is None else [pinned(incoming)]

        def body(arenas, *refs):
            *given, send = refs
            core = lax.rem(lax.axis_index("dp"), 2)
            if given:
                @pl.when(lax.axis_index("section") == 0)
                def _():
                    self.layout.views(arenas)(G_LOW, 1)[...] = given[0][...]

            if self.extra:
                view = self.layout.views(arenas)
                sums = view(SUMS, 0)[...] + view(SUMS, 1)[...]
                for pair in range(self.pairs):
                    low, high = (
                        spread(sums, 2 * pair + half, 2 * self.pairs, self.layout.hidden, self.columns) for half in range(2)
                    )
                    for target, half in ((self.block(arenas, pair), core), (send.at[pair], 1 - core)):
                        target[self.own :, :] = jnp.where(half == 0, low, high).astype(BF)

            per = min(self.per, self.pairs)
            for start in range(0, self.pairs, per):
                rows = pl.ds(2 * start * self.own, 2 * per * self.own)
                total = None
                for slot in range(2):
                    view = self.layout.views(arenas, slot)
                    term = dot_tn(view(self.left)[:, rows], view(self.right)[:, self.lanes])
                    total = term if total is None else total + term
                total = total.astype(BF).reshape(per, 2, self.own, self.columns)
                for j in range(per):
                    self.block(arenas, start + j)[: self.own, :] = jnp.where(core == 0, total[j, 0], total[j, 1])
                    send[start + j, : self.own, :] = jnp.where(core == 0, total[j, 1], total[j, 0])

        arenas, (send,) = run(
            body, arenas, self.layout, ins=ins, in_specs=[VM] * len(ins),
            outs=[pltpu.VMEM((self.pairs, self.rows, self.columns), BF)], out_specs=[VM], name="product",
        )
        self.moved = exchanged(send, 1)
        return arenas

    def step(self, arenas, totals):
        free, done = list(self.free), [place for place in range(self.pairs.bit_length() - 1) if place not in self.free]
        bit = self.todo.pop(0) if self.todo else None
        place = None if bit is None else bit.bit_length() - 2
        rest = [p for p in free if p != place]
        earlier = totals.get(self.name) if place is None else None

        def body(arenas, moved, *refs):
            device = lax.axis_index("dp")

            def mine(place):
                return lax.rem(lax.div(device, 2 << place), 2)

            base = sum((mine(p) << p for p in done), 0)

            def spot(number, side):
                bits = {p: (number >> k) & 1 for k, p in enumerate(rest)}
                if place is not None:
                    bits[place] = side
                index = sum((bits[p] << k for k, p in enumerate(free)), 0)
                return base + sum((bits[p] << p for p in free), 0), index

            if place is None:
                pair, index = spot(0, None)
                total = self.block(arenas, pair)[...].astype(F32) + moved[index].astype(F32)
                self.finish(total, *refs[0 if earlier is None else 1 :])
                return
            target, side = refs[0], mine(place)
            for number in range(1 << len(rest)):
                pair, index = spot(number, 1 - side)
                target[number] = self.block(arenas, pair)[...] + moved[index]
                pair, index = spot(number, side)
                block = self.block(arenas, pair)
                block[...] = block[...] + moved[index]

        ins = [] if earlier is None else [in_hbm(earlier)]
        if place is None:
            share = self.layout.width // (2 * self.pairs)
            outs, out_specs = [jax.ShapeDtypeStruct((self.own, self.full), F32)], [HB]
            scratch = [pltpu.VMEM((self.own, self.columns), F32), pltpu.SemaphoreType.DMA]
            if self.extra:
                outs += [jax.ShapeDtypeStruct((1, n, share), F32) for n in (2, 2, 4)]
                outs += [jax.ShapeDtypeStruct((1, self.layout.hidden // (2 * self.pairs)), F32)]
                out_specs += [VM] * 4
        else:
            outs, out_specs, scratch = [pltpu.VMEM((1 << len(rest), self.rows, self.columns), BF)], [VM], []
        arenas, results = run(
            body, arenas, self.layout, ins=[pinned(self.moved), *ins], in_specs=[VM] + [HB] * len(ins), outs=outs,
            out_specs=out_specs, scratch=scratch, name="add", weight=30, aliases={1: 0} if ins else {},
        )
        if place is None:
            totals[self.name] = results[0]
            if self.extra:
                totals[None] = results[1:]
        else:
            self.moved = exchanged(results[0], bit)
            self.free = rest
        return arenas

    def finish(self, total, *refs):
        *refs, held, sem = refs
        held[...] = total[: self.own]
        copy = pltpu.make_async_copy(held, refs[0].at[:, self.lanes], sem)
        copy.start()
        if self.extra:
            small, start = total[self.own :], 0
            for target in refs[1:4]:
                count, share = target.shape[1:]
                target[0] = small[start : start + count, :share]
                start += count
            refs[4][...] = small[8:9, : refs[4].shape[1]]
        copy.wait()


def shifted(value, axis, by):
    devices = lax.axis_size(axis)
    pairs = [(i, i + by) for i in range(devices) if 0 <= i + by < devices]
    return lax.ppermute(value, axis, pairs)


def exchanged(value, bit):
    return lax.ppermute(value, "dp", [(i, i ^ bit) for i in range(lax.axis_size("dp"))])


UP, SIDE = (2, 4, 8), (4, 8, 2)
PARTS = (
    (REDUCE, 0, 2, UP), (REDUCE, 1, 2, UP), (EXPAND, 0, 2, UP), (EXPAND, 1, 2, SIDE), (ATTEND, 0, 2, UP), (ATTEND, 1, 2, UP), (OUTPUT, 0, 1, UP)
)
OUTER, INNER, EDGES = -1, -2, -3
TURNS = (1, OUTER, 1, 3, 2, 3, 0, 2, INNER, 4, 1, 3, 4, EDGES, 2, 1, 0, 4, 2, 3, 1, 5, 0, 5, 3, 6, 4, 6, 0, 5, 4, 2, 6, 0, 5, 6, 5, 6)


def shards(
    ends, lengths, norm_gains, norm_shifts, attend_weight, offsets, output_weight, expand_weight, expand_bias, reduce_weight
):
    devices = lax.axis_size("dp")
    count, width = ends.shape[2:]
    hidden = expand_weight.shape[2]
    layout = Layout(count, width, hidden)
    small = (norm_gains, norm_shifts, offsets, expand_bias)
    weights = (attend_weight, output_weight, expand_weight, reduce_weight)

    arenas, (low,) = forward_first(layout, ends, lengths, small, weights)
    incoming = shifted(low, "section", 1)
    arenas, (low,) = forward_later(layout, arenas, 1, 0, 1, ends)
    later = shifted(low, "section", 1)
    arenas, _ = forward_later(layout, arenas, 1, 1, 0, ends, incoming)
    arenas = backward_outer(layout, arenas, 1, 1)
    arenas, (low,) = backward_inner(layout, arenas, 1, 1)
    grad_zero = shifted(low, "section", -1)
    arenas, _ = forward_later(layout, arenas, 0, 1, 1, ends, later, True)
    arenas = backward_outer(layout, arenas, 0, 1)
    arenas, (low,) = backward_inner(layout, arenas, 0, 1)
    grad_one = shifted(low, "section", -1)
    arenas = backward_outer(layout, arenas, 0, 0, grad_zero)
    arenas, _ = backward_inner(layout, arenas, 0, 0)

    if devices == 16:
        shares = [Share(layout, devices, *part) for part in PARTS]
        made, totals = set(), {}
        for turn in TURNS:
            if turn == OUTER:
                arenas = backward_outer(layout, arenas, 1, 0, grad_one)
            elif turn == INNER:
                arenas, _ = backward_inner(layout, arenas, 1, 0)
            elif turn == EDGES:
                arenas, edges = edges_of(layout, arenas)
            elif turn in made:
                arenas = shares[turn].step(arenas, totals)
            else:
                arenas = shares[turn].make(arenas, None if made else grad_one)
                made.add(turn)
        gains, shifts, offset_grads, bias = totals[None]
        grads = {name: totals[name].T[None] for name in FACTORS}
    else:
        arenas = backward_outer(layout, arenas, 1, 0, grad_one)
        arenas, _ = backward_inner(layout, arenas, 1, 0)
        arenas, edges = edges_of(layout, arenas)
        sums = layout.cut(arenas, SUMS, 0) + layout.cut(arenas, SUMS, 1)
        grads = {}
        for name, (left, right, _) in FACTORS.items():
            term = sum(dot_tn(layout.cut(arenas, right, s), layout.cut(arenas, left, s)) for s in range(2)).astype(BF)
            grads[name] = lax.psum_scatter(term, "dp", scatter_dimension=1, tiled=True).astype(F32)[None]
        bias = sums[8 : 8 + hidden // width].reshape(width, hidden // width)
        little = lax.psum_scatter(jnp.concatenate([sums[:8].T, bias], axis=1), "dp", scatter_dimension=0, tiled=True)
        gains, shifts, offset_grads = (little[:, i:j].T[None] for i, j in ((0, 2), (2, 4), (4, 8)))
        bias = little[:, 8:].reshape(1, -1)
    return edges, gains, shifts, grads[ATTEND], offset_grads, grads[OUTPUT], grads[EXPAND], bias, grads[REDUCE]


def solution(mesh):
    in_specs = (
        P("section", None, "dp", None),
        P(None, "dp", None),
        P("section", None, None),
        P("section", None, None),
        P("section", None, None),
        P("section", None, None),
        P("section", None, None),
        P("section", None, None),
        P("section", None),
        P("section", None, None),
    )
    out_specs = (
        P("section", None, "dp", None),
        P("section", None, "dp"),
        P("section", None, "dp"),
        P("section", None, "dp"),
        P("section", None, "dp"),
        P("section", None, "dp"),
        P("section", None, "dp"),
        P("section", "dp"),
        P("section", None, "dp"),
    )
    return jax.shard_map(shards, mesh=mesh, in_specs=in_specs, out_specs=out_specs, check_vma=False)
```

```python
import jax
import jax.numpy as jnp
from jax import lax
from jax.experimental import pallas as pl
from jax.experimental.pallas import tpu as pltpu
from jax.sharding import PartitionSpec as P

HEADS = 12
ROWS = 32
LIMIT = 7 * 2**20
BF = jnp.bfloat16
F32 = jnp.float32
VM = pl.BlockSpec(memory_space=pltpu.VMEM)
HB = pl.BlockSpec(memory_space=pltpu.HBM)

SLOTTED = (
    FIRST, MIXED, SECOND, G_LOW, RESID_LOW, JOINED, GRAD_JOINED, SLOPE, WEIGHTS, ACT, PRE_LOW, UNIT, UNIT_TWO, EDGE, RATIO, SUMS
) = range(16)
SHARED = OUTPUT_W, REDUCE_W, GRAD_MIXED, ATTEND_W, EXPAND_W, GRAD_RESID, MIXTURE, PARAMS = range(16, 24)
REDUCE, EXPAND, ATTEND, OUTPUT = range(4)


def in_hbm(value):
    return pltpu.with_memory_space_constraint(value, pltpu.HBM)


def pinned(value):
    return pltpu.with_memory_space_constraint(value, pltpu.VMEM)


def dot(left, right, dims=((1,), (0,))):
    return lax.dot_general(left, right, (dims, ((), ())), preferred_element_type=F32)


def dot_nt(left, right):
    return dot(left, right, ((1,), (1,)))


def dot_tn(left, right):
    return dot(left, right, ((0,), (0,)))


class Layout:
    def __init__(self, count, width, hidden):
        self.count, self.width, self.hidden = count, width, hidden
        self.place, self.size = {}, [0, 0, 0, 0]
        self.lanes = (width, 3 * width, hidden, width)
        self.put(0, OUTPUT_W, width)
        self.put(0, REDUCE_W, hidden)
        self.put(0, GRAD_MIXED, count)
        self.put(1, ATTEND_W, width)
        self.put(2, EXPAND_W, width)
        self.put(3, GRAD_RESID, count)
        self.put(3, MIXTURE, count)
        self.put(3, PARAMS, 16)
        for slot in range(2):
            for name in (FIRST, MIXED, SECOND, G_LOW, RESID_LOW):
                self.put(0, (name, slot), count)
            for name in (JOINED, GRAD_JOINED):
                self.put(1, (name, slot), count)
            for name in (SLOPE, WEIGHTS, ACT, PRE_LOW):
                self.put(2, (name, slot), count)
            for name in (UNIT, UNIT_TWO, EDGE, RATIO):
                self.put(3, (name, slot), count)
            self.put(3, (SUMS, slot), 16)
        self.room = {
            REDUCE: self.place[SLOPE, 0][:2],
            EXPAND: self.place[REDUCE_W][:2],
            ATTEND: (0, self.place[REDUCE_W][1] + hidden // 2),
            OUTPUT: self.place[OUTPUT_W][:2],
        }

    def put(self, arena, name, rows):
        self.place[name] = (arena, self.size[arena], rows)
        self.size[arena] += rows

    def shapes(self):
        return [pltpu.VMEM((rows, lanes), F32 if i == 3 else BF) for i, (rows, lanes) in enumerate(zip(self.size, self.lanes))]

    def views(self, arenas, slot=None):
        def view(name, slot=slot):
            arena, start, rows = self.place[name if name in self.place else (name, slot)]
            return arenas[arena].at[pl.ds(start, rows), :]

        return view

    def cut(self, arenas, name, slot):
        arena, start, rows = self.place[name, slot]
        return arenas[arena][start : start + rows]

    def lanes_of(self, name):
        return self.lanes[self.place[name, 0][0]]


def run(body, arenas, layout, ins=(), in_specs=(), outs=(), out_specs=(), scratch=(), name=None, weight=0, aliases=None):
    held = [] if arenas is None else [pinned(arena) for arena in arenas]
    given, kept = len(held) + len(ins), len(layout.lanes)

    def kernel(*refs):
        body(refs[given : given + kept], *refs[len(held) : given], *refs[given + kept :])

    result = pl.pallas_call(
        kernel,
        out_shape=layout.shapes() + list(outs),
        in_specs=[VM] * len(held) + list(in_specs),
        out_specs=[VM] * kept + list(out_specs),
        scratch_shapes=list(scratch),
        input_output_aliases={
            **{i: i for i in range(len(held))}, **{len(held) + i: kept + o for i, o in (aliases or {}).items()}
        },
        compiler_params=pltpu.CompilerParams(vmem_limit_bytes=LIMIT),
        cost_estimate=pl.CostEstimate(flops=1 + weight * 10**9, bytes_accessed=0, transcendentals=0),
        name=name,
    )(*held, *ins)
    return list(result[:kept]), list(result[kept:])


def group_bias(lengths_ref, micro, count):
    rows = lax.broadcasted_iota(jnp.int32, (count, count), 0)
    cols = lax.broadcasted_iota(jnp.int32, (count, count), 1)
    bound = jnp.int32(0)
    row_group = jnp.zeros((count, count), jnp.int32)
    col_group = jnp.zeros((count, count), jnp.int32)
    for crop in range(lengths_ref.shape[2]):
        bound = bound + lengths_ref[micro, 0, crop]
        row_group = row_group + (rows >= bound).astype(jnp.int32)
        col_group = col_group + (cols >= bound).astype(jnp.int32)
    return jnp.where(row_group == col_group, 0.0, -1e30).astype(F32)


def gelu_parts(pre):
    upper = 0.5 * (1.0 + lax.erf(pre * (2.0 ** -0.5)))
    return pre * upper, upper + pre * (jnp.exp(-0.5 * pre * pre) * 0.3989422804014327)


def norm_rows(values):
    center = values - jnp.mean(values, axis=-1, keepdims=True)
    factor = lax.rsqrt(jnp.mean(center * center, axis=-1, keepdims=True) + 1e-06)
    return center * factor, factor


def halves(count):
    lane = lax.broadcasted_iota(jnp.int32, (count, 128), 1)
    return lane < 64, lane >= 64


def factor_column(count, slot, norm):
    column = 2 * count + 128 * slot + norm
    return slice(column, column + 1)


def forward_body(view, slot, micro, a, low, ready):
    count, width = a.shape
    first, joined, kept, mixed, act, slope = (view(n) for n in (FIRST, JOINED, WEIGHTS, MIXED, ACT, SLOPE))
    ratio = view(RATIO)
    unit, unit_two, out, second, mixture, params = (view(n) for n in (UNIT, UNIT_TWO, EDGE, SECOND, MIXTURE, PARAMS))
    attend_w, output_w, expand_w, reduce_w = (view(n) for n in (ATTEND_W, OUTPUT_W, EXPAND_W, REDUCE_W))
    hidden = act.shape[1]
    bias = pl.ds(micro * count, count)

    def norm(source, unit, target, index):
        gain, shift = params[index : index + 1, :], params[2 + index : 3 + index, :]
        for r in range(0, count, ROWS):
            rows = pl.ds(r, ROWS)
            normed, factor = norm_rows(source[rows, :])
            unit[rows, :] = normed
            mixture[rows, factor_column(count, slot, index)] = factor
            target[rows, :] = (normed * gain + shift).astype(BF)

    ready(PARAMS, 0)
    norm(a, unit, first, 0)
    for i in range(3):
        ready(ATTEND_W, i)
        cols = pl.ds(i * width, width)
        part = dot(first[...], attend_w[:, cols])
        if i == 0:
            part = part + params[4:5, :]
        if i == 2:
            part = part + params[5:6, :]
        joined[:, cols] = part.astype(BF)

    ready(MIXTURE, 0)
    sides = halves(count)
    for pair in range(HEADS // 2):
        query = joined[:, pl.ds(pair * 128, 128)] * (64 ** -0.5)
        key = joined[:, pl.ds(width + pair * 128, 128)]
        value = joined[:, pl.ds(2 * width + pair * 128, 128)]
        value = jnp.concatenate([value, jnp.ones((count, 128), BF)], axis=1)
        sums = []
        for half in range(2):
            scores = dot_nt(jnp.where(sides[half], query, 0).astype(BF), key) + mixture[:, bias]
            weights = jnp.exp(scores - jnp.max(scores, axis=-1, keepdims=True)).astype(BF)
            kept[:, pl.ds((2 * pair + half) * count, count)] = weights
            sums.append(dot(weights, value))
        both = jnp.where(jnp.concatenate([sides[0]] * 2, axis=1), *sums)
        inverse = 1.0 / both[:, 128:]
        ratio[:, pl.ds(pair * 128, 128)] = inverse
        mixed[:, pl.ds(pair * 128, 128)] = (both[:, :128] * inverse).astype(BF)

    ready(OUTPUT_W, 0)
    out[...] = a[...] + dot(mixed[...], output_w[...]) + params[6:7, :]
    norm(out, unit_two, second, 1)
    for i in range(hidden // width):
        cols = pl.ds(i * width, width)
        ready(EXPAND_W, i)
        pre = dot(second[...], expand_w[:, cols]) + params[8 + i : 9 + i, :]
        value, grad = gelu_parts(pre)
        act[:, cols] = value.astype(BF)
        slope[:, cols] = grad.astype(BF)
        ready(REDUCE_W, i)
        out[...] += dot(act[:, cols], reduce_w[cols, :])
    out[...] += params[7:8, :]
    low[...] = out[...].astype(BF)


def forward_first(layout, ends, lengths, small, weights):
    count, width, hidden = layout.count, layout.width, layout.hidden
    tiles = hidden // width

    def body(arenas, ends, lengths, gains, shifts, offsets, bias, attend, output, expand, reduce, low, *scratch):
        a, lengths_s, gains_v, shifts_v, offsets_v, bias_v, sems, first_sems = scratch
        view = layout.views(arenas, 0)
        params, mixture = view(PARAMS), view(MIXTURE)
        attend_w, output_w, expand_w, reduce_w = (view(n) for n in (ATTEND_W, OUTPUT_W, EXPAND_W, REDUCE_W))
        early = [
            pltpu.make_async_copy(source, target, first_sems.at[i])
            for i, (source, target) in enumerate(
                [
                    (ends.at[0, 0], a), (gains, gains_v), (shifts, shifts_v), (lengths, lengths_s),
                    (offsets, offsets_v), (bias, bias_v),
                ]
            )
        ]
        copies = {}
        for i in range(3):
            cols = pl.ds(i * width, width)
            copies[ATTEND_W, i] = attend.at[0, :, cols], attend_w.at[:, cols]
        copies[OUTPUT_W, 0] = output.at[0], output_w
        for i in range(tiles):
            cols = pl.ds(i * width, width)
            copies[EXPAND_W, i] = expand.at[0, :, cols], expand_w.at[:, cols]
            copies[REDUCE_W, i] = reduce.at[0, cols], reduce_w.at[cols, :]
        for number, (name, pair) in enumerate(copies.items()):
            copies[name] = pltpu.make_async_copy(*pair, sems.at[number])
        order = list(copies)
        for copy in early:
            copy.start()
        for name in order[:4]:
            copies[name].start()
        middle = 4 + tiles // 2 * 2
        awaited = {(ATTEND_W, 0): order[:3], (OUTPUT_W, 0): order[3:middle], (EXPAND_W, tiles // 2): order[middle:]}

        def ready(name, i):
            if name == PARAMS:
                for copy in early:
                    copy.wait()
                params[0:2, :] = gains_v[0]
                params[2:4, :] = shifts_v[0]
                params[4:8, :] = offsets_v[0]
                for tile in range(tiles):
                    params[8 + tile : 9 + tile, :] = bias_v[0:1, pl.ds(tile * width, width)]
            elif name == MIXTURE:
                for micro in range(lengths.shape[0]):
                    mixture[:, pl.ds(micro * count, count)] = group_bias(lengths_s, micro, count)
            else:
                for each in awaited.get((name, i), ()):
                    copies[each].wait()
                if (name, i) == (ATTEND_W, 0):
                    for later in order[4:]:
                        copies[later].start()

        section = lax.axis_index("section")
        pl.when(section == 0)(lambda: forward_body(view, 0, 0, a, low, ready))

        @pl.when(section != 0)
        def _():
            for name in ((PARAMS, 0), (MIXTURE, 0), *order):
                ready(*name)
            view(UNIT)[...] = a[...]

    return run(
        body, None, layout,
        ins=[in_hbm(v) for v in (ends, lengths, *small, *weights)], in_specs=[HB] * 10,
        outs=[pltpu.VMEM((count, width), BF)], out_specs=[VM],
        scratch=[
            pltpu.VMEM((count, width), F32), pltpu.SMEM(lengths.shape, jnp.int32),
            *[pltpu.VMEM(v.shape, F32) for v in small],
            pltpu.SemaphoreType.DMA((4 + 2 * tiles,)), pltpu.SemaphoreType.DMA((6,)),
        ],
        name="forward_first",
    )


def forward_later(layout, arenas, slot, side, micro, ends, incoming=None, take=False):
    count, width = layout.count, layout.width
    ins = [in_hbm(ends)] + ([] if incoming is None else [pinned(incoming)])

    def body(arenas, ends, *refs):
        *given, low, a, sem = refs
        view = layout.views(arenas, slot)

        def step():
            forward_body(view, slot, micro, a, low, lambda name, i: None)

        @pl.when(lax.axis_index("section") == side)
        def _():
            if not given:
                copy = pltpu.make_async_copy(ends.at[0, micro], a, sem)
                copy.start()
                copy.wait()
                step()
                return
            if take:
                copy = pltpu.make_async_copy(ends.at[0, ends.shape[1] - 1], view(UNIT, 1 - slot), sem)
                copy.start()
            a[...] = given[0][...].astype(F32)
            step()
            if take:
                copy.wait()

    return run(
        body, arenas, layout, ins=ins, in_specs=[HB, VM][: len(ins)],
        outs=[pltpu.VMEM((count, width), BF)], out_specs=[VM],
        scratch=[pltpu.VMEM((count, width), F32), pltpu.SemaphoreType.DMA], name="forward_later",
    )


def norm_back_all(grad, gain, normed_ref, factors, base, emit):
    count, width = normed_ref.shape
    sums = [jnp.zeros((8, width), F32)] * 3

    def fold(values):
        return jnp.sum(values.reshape(-1, 8, width), axis=0)

    for r in range(0, count, ROWS):
        rows = pl.ds(r, ROWS)
        part, normed = grad[rows, :], normed_ref[rows, :]
        scaled = part * gain
        result = base(rows) + factors(rows) * (
            scaled
            - jnp.mean(scaled, axis=-1, keepdims=True)
            - normed * jnp.mean(scaled * normed, axis=-1, keepdims=True)
        )
        sums = [total + fold(term) for total, term in zip(sums, (part * normed, part, result))]
        emit(rows, result)
    return [column_sum(total) for total in sums]


def column_sum(values):
    return jnp.sum(values, axis=0, keepdims=True)


def outer_body(view, slot, g, grad_second):
    count, width = g.shape
    slope, pre_low, g_low, resid_low, sums = (view(n) for n in (SLOPE, PRE_LOW, G_LOW, RESID_LOW, SUMS))
    grad_resid, mixture, params = view(GRAD_RESID), view(MIXTURE), view(PARAMS)
    output_w, expand_w, reduce_w = view(OUTPUT_W), view(EXPAND_W), view(REDUCE_W)
    hidden = slope.shape[1]
    g_low[...] = g[...].astype(BF)
    sums[7:8, :] = column_sum(g[...])
    for i in range(hidden // width):
        cols = pl.ds(i * width, width)
        grad_pre = dot_nt(g_low[...], reduce_w[cols, :]) * slope[:, cols].astype(F32)
        sums[8 + i : 9 + i, :] = column_sum(grad_pre)
        pre_low[:, cols] = grad_pre.astype(BF)
        term = dot_nt(pre_low[:, cols], expand_w[:, cols])
        if i == 0:
            grad_second[...] = term
        else:
            grad_second[...] += term

    def emit(rows, result):
        grad_resid[rows, :] = result
        resid_low[rows, :] = result.astype(BF)

    sums[1:2, :], sums[3:4, :], sums[6:7, :] = norm_back_all(
        grad_second, params[1:2, :], view(UNIT_TWO), lambda rows: mixture[rows, factor_column(count, slot, 1)],
        lambda rows: g[rows, :], emit,
    )
    view(GRAD_MIXED)[...] = dot_nt(resid_low[...], output_w[...]).astype(BF)


def inner_body(view, slot, low, grad_first):
    grad_resid, grad_mixed, joined, kept = view(GRAD_RESID), view(GRAD_MIXED), view(JOINED), view(WEIGHTS)
    mixed, ratio = view(MIXED), view(RATIO)
    grad_joined, edge, sums = view(GRAD_JOINED), view(EDGE), view(SUMS)
    mixture, params, attend_w = view(MIXTURE), view(PARAMS), view(ATTEND_W)
    first_layer = lax.axis_index("section") == 0
    count, width = grad_resid.shape
    sides = halves(count)
    for pair in range(HEADS // 2):
        at = [pl.ds(j * width + pair * 128, 128) for j in range(3)]
        query, key, value = joined[:, at[0]] * (64 ** -0.5), joined[:, at[1]] * (64 ** -0.5), joined[:, at[2]]
        grad_out = grad_mixed[:, at[0]].astype(F32) * ratio[:, at[0]]
        inner = -grad_out * mixed[:, at[0]].astype(F32)
        value = jnp.concatenate([value, jnp.ones((count, 128), BF)], axis=1)
        totals = [None] * 3
        for half in range(2):
            side = sides[half]
            weights = kept[:, pl.ds((2 * pair + half) * count, count)]
            grad_half = jnp.where(side, grad_out, 0).astype(BF)
            part = jnp.concatenate([grad_half, jnp.where(side, inner, 0).astype(BF)], axis=1)
            grad_score = (weights.astype(F32) * dot_nt(part, value)).astype(BF)
            terms = (
                dot(grad_score, jnp.where(side, key, 0).astype(BF)),
                dot_tn(grad_score, jnp.where(side, query, 0).astype(BF)),
                dot_tn(weights, grad_half),
            )
            totals = [t if old is None else old + t for old, t in zip(totals, terms)]
        for j in range(3):
            grad_joined[:, at[j]] = totals[j].astype(BF)
    sums[4:5, :] = column_sum(grad_joined[:, pl.ds(0, width)].astype(F32))
    sums[5:6, :] = column_sum(grad_joined[:, pl.ds(2 * width, width)].astype(F32))
    grad_first[...] = dot_nt(grad_joined[...], attend_w[...])

    def emit(rows, result):
        edge[rows, :] = jnp.where(first_layer, result, edge[rows, :])
        low[rows, :] = result.astype(BF)

    sums[0:1, :], sums[2:3, :], _ = norm_back_all(
        grad_first, params[0:1, :], view(UNIT), lambda rows: mixture[rows, factor_column(count, slot, 0)],
        lambda rows: grad_resid[rows, :], emit,
    )


def backward_outer(layout, arenas, slot, side, incoming=None):
    count, width = layout.count, layout.width
    ins = [] if incoming is None else [pinned(incoming)]

    def body(arenas, *refs):
        *given, g, grad_second = refs
        view = layout.views(arenas, slot)

        @pl.when(lax.axis_index("section") == side)
        def _():
            g[...] = given[0][...].astype(F32) if given else view(UNIT, 1 - slot)[...]
            outer_body(view, slot, g, grad_second)

    return run(
        body, arenas, layout, ins=ins, in_specs=[VM] * len(ins),
        scratch=[pltpu.VMEM((count, width), F32), pltpu.VMEM((count, width), F32)], name="backward_outer",
    )[0]


def backward_inner(layout, arenas, slot, side):
    count, width = layout.count, layout.width

    def body(arenas, low, grad_first):
        @pl.when(lax.axis_index("section") == side)
        def _():
            inner_body(layout.views(arenas, slot), slot, low, grad_first)

    return run(
        body, arenas, layout, outs=[pltpu.VMEM((count, width), BF)], out_specs=[VM],
        scratch=[pltpu.VMEM((count, width), F32)], name="backward_inner",
    )


def backward(layout, arenas, slot, side, incoming=None):
    count, width = layout.count, layout.width
    ins = [] if incoming is None else [pinned(incoming)]

    def body(arenas, *refs):
        *given, low, g, grad = refs
        view = layout.views(arenas, slot)

        @pl.when(lax.axis_index("section") == side)
        def _():
            g[...] = given[0][...].astype(F32) if given else view(UNIT, 1 - slot)[...]
            outer_body(view, slot, g, grad)
            inner_body(view, slot, low, grad)

    return run(
        body, arenas, layout, ins=ins, in_specs=[VM] * len(ins),
        outs=[pltpu.VMEM((count, width), BF)], out_specs=[VM],
        scratch=[pltpu.VMEM((count, width), F32), pltpu.VMEM((count, width), F32)], name="backward",
    )


def edges_of(layout, arenas):
    def body(arenas, edges, sems):
        view = layout.views(arenas)

        def move(slots):
            copies = [pltpu.make_async_copy(view(EDGE, slot), edges.at[0, i], sems.at[i]) for i, slot in enumerate(slots)]
            for copy in copies:
                copy.start()
            for copy in copies:
                copy.wait()

        section = lax.axis_index("section")
        pl.when(section == 0)(lambda: move((0, 1)))
        pl.when(section != 0)(lambda: move((1, 0)))

    arenas, (edges,) = run(
        body, arenas, layout, outs=[jax.ShapeDtypeStruct((1, 2, layout.count, layout.width), F32)], out_specs=[HB],
        scratch=[pltpu.SemaphoreType.DMA((2,))], name="edges",
    )
    return arenas, edges


FACTORS = {
    REDUCE: (G_LOW, ACT, 8), EXPAND: (PRE_LOW, SECOND, 2), ATTEND: (GRAD_JOINED, FIRST, 4), OUTPUT: (RESID_LOW, MIXED, 8)
}


def spread(sums, place, devices, hidden, lanes):
    width = sums.shape[1]
    share, wide = width // devices, hidden // devices
    bias = 8 + place * wide // width
    rows = (sums[:8], jnp.broadcast_to(sums[bias : bias + 1], (8, width)))
    starts = (place * share, place * wide % width)
    return jnp.concatenate([pltpu.roll(row, (width - start) % width, 1) for row, start in zip(rows, starts)])[:, :lanes]


class Share:
    def __init__(self, layout, devices, name, part, parts, order):
        left, right, self.per = FACTORS[name]
        self.layout, self.name, self.left, self.right = layout, name, left, right
        self.extra = name == ATTEND and part == 0
        self.own = layout.lanes_of(left) // devices
        self.rows = self.own + (16 if self.extra else 0)
        self.full = layout.lanes_of(right)
        self.columns = self.full // parts
        self.lanes = pl.ds(part * self.columns, self.columns)
        self.pairs = devices // 2
        self.todo, self.free = list(order), list(range(self.pairs.bit_length() - 1))
        self.total = None

    def block(self, arenas, pair):
        arena, start = self.layout.room[self.name]
        row = start + pair * (self.own + (16 if self.name == ATTEND else 0))
        return arenas[arena].at[pl.ds(row if isinstance(row, int) else pl.multiple_of(row, 16), self.rows), self.lanes]

    def make(self, arenas, incoming=None):
        ins = [] if incoming is None else [pinned(incoming)]

        def body(arenas, *refs):
            *given, send = refs
            core = lax.rem(lax.axis_index("dp"), 2)
            if given:
                @pl.when(lax.axis_index("section") == 0)
                def _():
                    self.layout.views(arenas)(G_LOW, 1)[...] = given[0][...]

            if self.extra:
                view = self.layout.views(arenas)
                sums = view(SUMS, 0)[...] + view(SUMS, 1)[...]
                for pair in range(self.pairs):
                    low, high = (
                        spread(sums, 2 * pair + half, 2 * self.pairs, self.layout.hidden, self.columns) for half in range(2)
                    )
                    for target, half in ((self.block(arenas, pair), core), (send.at[pair], 1 - core)):
                        target[self.own :, :] = jnp.where(half == 0, low, high).astype(BF)

            per = min(self.per, self.pairs)
            for start in range(0, self.pairs, per):
                rows = pl.ds(2 * start * self.own, 2 * per * self.own)
                total = None
                for slot in range(2):
                    view = self.layout.views(arenas, slot)
                    term = dot_tn(view(self.left)[:, rows], view(self.right)[:, self.lanes])
                    total = term if total is None else total + term
                total = total.astype(BF).reshape(per, 2, self.own, self.columns)
                for j in range(per):
                    self.block(arenas, start + j)[: self.own, :] = jnp.where(core == 0, total[j, 0], total[j, 1])
                    send[start + j, : self.own, :] = jnp.where(core == 0, total[j, 1], total[j, 0])

        arenas, (send,) = run(
            body, arenas, self.layout, ins=ins, in_specs=[VM] * len(ins),
            outs=[pltpu.VMEM((self.pairs, self.rows, self.columns), BF)], out_specs=[VM], name="product",
        )
        self.moved = exchanged(send, 1)
        return arenas

    def step(self, arenas, totals):
        free, done = list(self.free), [place for place in range(self.pairs.bit_length() - 1) if place not in self.free]
        bit = self.todo.pop(0) if self.todo else None
        place = None if bit is None else bit.bit_length() - 2
        rest = [p for p in free if p != place]
        earlier = totals.get(self.name) if place is None else None

        def body(arenas, moved, *refs):
            device = lax.axis_index("dp")

            def mine(place):
                return lax.rem(lax.div(device, 2 << place), 2)

            base = sum((mine(p) << p for p in done), 0)

            def spot(number, side):
                bits = {p: (number >> k) & 1 for k, p in enumerate(rest)}
                if place is not None:
                    bits[place] = side
                index = sum((bits[p] << k for k, p in enumerate(free)), 0)
                return base + sum((bits[p] << p for p in free), 0), index

            if place is None:
                pair, index = spot(0, None)
                total = self.block(arenas, pair)[...].astype(F32) + moved[index].astype(F32)
                self.finish(total, *refs[0 if earlier is None else 1 :])
                return
            target, side = refs[0], mine(place)
            for number in range(1 << len(rest)):
                pair, index = spot(number, 1 - side)
                target[number] = self.block(arenas, pair)[...] + moved[index]
                pair, index = spot(number, side)
                block = self.block(arenas, pair)
                block[...] = block[...] + moved[index]

        ins = [] if earlier is None else [in_hbm(earlier)]
        if place is None:
            share = self.layout.width // (2 * self.pairs)
            outs, out_specs = [jax.ShapeDtypeStruct((self.own, self.full), F32)], [HB]
            scratch = [pltpu.VMEM((self.own, self.columns), F32), pltpu.SemaphoreType.DMA]
            if self.extra:
                outs += [jax.ShapeDtypeStruct((1, n, share), F32) for n in (2, 2, 4)]
                outs += [jax.ShapeDtypeStruct((1, self.layout.hidden // (2 * self.pairs)), F32)]
                out_specs += [VM] * 4
        else:
            outs, out_specs, scratch = [pltpu.VMEM((1 << len(rest), self.rows, self.columns), BF)], [VM], []
        arenas, results = run(
            body, arenas, self.layout, ins=[pinned(self.moved), *ins], in_specs=[VM] + [HB] * len(ins), outs=outs,
            out_specs=out_specs, scratch=scratch, name="add", weight=16, aliases={1: 0} if ins else {},
        )
        if place is None:
            totals[self.name] = results[0]
            if self.extra:
                totals[None] = results[1:]
        else:
            self.moved = exchanged(results[0], bit)
            self.free = rest
        return arenas

    def finish(self, total, *refs):
        *refs, held, sem = refs
        held[...] = total[: self.own]
        copy = pltpu.make_async_copy(held, refs[0].at[:, self.lanes], sem)
        copy.start()
        if self.extra:
            small, start = total[self.own :], 0
            for target in refs[1:4]:
                count, share = target.shape[1:]
                target[0] = small[start : start + count, :share]
                start += count
            refs[4][...] = small[8:9, : refs[4].shape[1]]
        copy.wait()


def shifted(value, axis, by):
    devices = lax.axis_size(axis)
    pairs = [(i, i + by) for i in range(devices) if 0 <= i + by < devices]
    return lax.ppermute(value, axis, pairs)


def exchanged(value, bit):
    return lax.ppermute(value, "dp", [(i, i ^ bit) for i in range(lax.axis_size("dp"))])


UP, SIDE = (2, 4, 8), (4, 8, 2)
PARTS = (
    (REDUCE, 0, 2, UP), (REDUCE, 1, 2, UP), (EXPAND, 0, 2, UP), (EXPAND, 1, 2, SIDE), (ATTEND, 0, 2, UP), (ATTEND, 1, 2, UP), (OUTPUT, 0, 1, UP)
)
OUTER, INNER, EDGES = -1, -2, -3
TURNS = (1, OUTER, 1, 3, 2, 3, 0, 2, INNER, 4, 1, 3, 4, EDGES, 2, 0, 1, 4, 2, 3, 1, 5, 0, 5, 3, 6, 4, 2, 6, 0, 5, 6, 0, 5, 6, 4, 5, 6)


def shards(
    ends, lengths, norm_gains, norm_shifts, attend_weight, offsets, output_weight, expand_weight, expand_bias, reduce_weight
):
    devices = lax.axis_size("dp")
    count, width = ends.shape[2:]
    hidden = expand_weight.shape[2]
    layout = Layout(count, width, hidden)
    small = (norm_gains, norm_shifts, offsets, expand_bias)
    weights = (attend_weight, output_weight, expand_weight, reduce_weight)

    arenas, (low,) = forward_first(layout, ends, lengths, small, weights)
    incoming = shifted(low, "section", 1)
    arenas, (low,) = forward_later(layout, arenas, 1, 0, 1, ends)
    later = shifted(low, "section", 1)
    arenas, _ = forward_later(layout, arenas, 1, 1, 0, ends, incoming)
    arenas, (low,) = backward(layout, arenas, 1, 1)
    grad_zero = shifted(low, "section", -1)
    arenas, _ = forward_later(layout, arenas, 0, 1, 1, ends, later, True)
    arenas, (low,) = backward(layout, arenas, 0, 1)
    grad_one = shifted(low, "section", -1)
    arenas, _ = backward(layout, arenas, 0, 0, grad_zero)

    if devices == 16:
        shares = [Share(layout, devices, *part) for part in PARTS]
        made, totals = set(), {}
        for turn in TURNS:
            if turn == OUTER:
                arenas = backward_outer(layout, arenas, 1, 0, grad_one)
            elif turn == INNER:
                arenas, _ = backward_inner(layout, arenas, 1, 0)
            elif turn == EDGES:
                arenas, edges = edges_of(layout, arenas)
            elif turn in made:
                arenas = shares[turn].step(arenas, totals)
            else:
                arenas = shares[turn].make(arenas, None if made else grad_one)
                made.add(turn)
        gains, shifts, offset_grads, bias = totals[None]
        grads = {name: totals[name].T[None] for name in FACTORS}
    else:
        arenas = backward_outer(layout, arenas, 1, 0, grad_one)
        arenas, _ = backward_inner(layout, arenas, 1, 0)
        arenas, edges = edges_of(layout, arenas)
        sums = layout.cut(arenas, SUMS, 0) + layout.cut(arenas, SUMS, 1)
        grads = {}
        for name, (left, right, _) in FACTORS.items():
            term = sum(dot_tn(layout.cut(arenas, right, s), layout.cut(arenas, left, s)) for s in range(2)).astype(BF)
            grads[name] = lax.psum_scatter(term, "dp", scatter_dimension=1, tiled=True).astype(F32)[None]
        bias = sums[8 : 8 + hidden // width].reshape(width, hidden // width)
        little = lax.psum_scatter(jnp.concatenate([sums[:8].T, bias], axis=1), "dp", scatter_dimension=0, tiled=True)
        gains, shifts, offset_grads = (little[:, i:j].T[None] for i, j in ((0, 2), (2, 4), (4, 8)))
        bias = little[:, 8:].reshape(1, -1)
    return edges, gains, shifts, grads[ATTEND], offset_grads, grads[OUTPUT], grads[EXPAND], bias, grads[REDUCE]


def solution(mesh):
    in_specs = (
        P("section", None, "dp", None),
        P(None, "dp", None),
        P("section", None, None),
        P("section", None, None),
        P("section", None, None),
        P("section", None, None),
        P("section", None, None),
        P("section", None, None),
        P("section", None),
        P("section", None, None),
    )
    out_specs = (
        P("section", None, "dp", None),
        P("section", None, "dp"),
        P("section", None, "dp"),
        P("section", None, "dp"),
        P("section", None, "dp"),
        P("section", None, "dp"),
        P("section", None, "dp"),
        P("section", "dp"),
        P("section", None, "dp"),
    )
    return jax.shard_map(shards, mesh=mesh, in_specs=in_specs, out_specs=out_specs, check_vma=False)
```
